256 devices in a mesh: ctx: 32 (over x, z), kv: 8 (over y, core).
Axes of the slice: x: 4, y: 4, z: 8, core: 2. Of those that a mesh axis runs over, the one named last changes fastest.
Arguments:
- ctx_query: bfloat16 [8, 16384, 1024], P('kv', 'ctx'), may hold values from -140 to 140
- ctx_kv: bfloat16 [2, 8, 16384, 128], P(None, 'kv', 'ctx'), may hold values from -6 to 6
- new_query: bfloat16 [8, 256, 1024], P('kv', 'ctx'), may hold values from -140 to 140
- new_kv: bfloat16 [2, 8, 256, 128], P(None, 'kv', 'ctx'), may hold values from -6 to 6
- out_weight: bfloat16 [8192, 8192], P('kv', 'ctx'), may hold values from -0.0625 to 0.0625
Outputs:
- ctx_out: bfloat16 [8, 16384, 1024], P('kv', 'ctx')
- new_out: bfloat16 [256, 8192], P('kv', 'ctx')
The draws below stay inside these ranges and needn't reach their ends.
All inputs are finite; a program needn't handle non-finite values.
Results may differ from the reference program's by a relative error of at most 0.0045.
Values may be sent and summed in bfloat16 or wider, within the bound.
A program may use at most 192 MiB of HBM per device.

```python
import jax
import jax.numpy as jnp
from jax import lax

HD = 128
GROUP = 8
D = 8192
BLK = 512
QTOK_DEV = 8
KV_HEADS = 8
CTX = 16384
QTOK = 256
N_CTX = 32


def context_keys(key):
    raw = jax.random.normal(jax.random.fold_in(key, 71), (KV_HEADS, CTX, HD), jnp.float32)
    return jnp.clip(raw, -6.0, 6.0)


def draw_ctx_kv(key, part):
    keys = context_keys(key)
    key = jax.random.fold_in(key, 3)
    values = jnp.clip(jax.random.normal(key, (KV_HEADS, CTX, HD), jnp.float32), -6.0, 6.0)
    return jnp.stack([keys, values]).astype(jnp.bfloat16)


def draw_ctx_query(key, part):
    key = jax.random.fold_in(key, 5)
    queries = jax.random.normal(key, (KV_HEADS, CTX, GROUP, HD), jnp.float32)
    return queries.reshape(KV_HEADS, CTX, GROUP * HD).astype(jnp.bfloat16)


def draw_new_query(key, part):
    key = jax.random.fold_in(key, 7)
    raw = jnp.clip(jax.random.normal(key, (KV_HEADS, QTOK, GROUP, HD), jnp.float32), -5.5, 5.5)
    queries = 24.0 * raw
    return queries.reshape(KV_HEADS, QTOK, GROUP * HD).astype(jnp.bfloat16)


def level_of(stream_key, shape, split, smallest, top_value):
    loudness, own = 1.0, jax.random.fold_in(stream_key, 6)
    for position, shards_of in split:
        steps = jnp.exp(jax.random.uniform(jax.random.fold_in(own, position), (shards_of,), jnp.float32, smallest / len(split), top_value / len(split)))
        loudness = loudness * jnp.repeat(steps, shape[position] // shards_of).reshape([-1 if axis == position else 1 for axis in range(len(shape))])
    return loudness


def scatter_about(stream_key, extent, deviation, limit, cuts=(), kind=jnp.bfloat16):
    loudness = level_of(stream_key, extent, cuts, -0.22, 0.18) if cuts else 1.0
    entries = jax.random.normal(stream_key, extent, jnp.float32) * deviation * loudness
    return jnp.minimum(jnp.maximum(entries, -limit), limit).astype(kind)


def setup_inputs(seed: int = 0) -> dict:
    seeds = jax.random.split(jax.random.key(seed), 6)
    ctx_query = draw_ctx_query(jax.random.fold_in(seeds[5], 71), 0)
    ctx_kv = draw_ctx_kv(jax.random.fold_in(seeds[5], 71), 0)
    new_query = draw_new_query(jax.random.fold_in(seeds[5], 71), 0)
    new_kv = scatter_about(seeds[3], (2, KV_HEADS, QTOK, HD), 1.0, 6.0, ((1, 8), (2, 32)))
    out_weight = scatter_about(seeds[4], (KV_HEADS * GROUP * HD, D), (KV_HEADS * GROUP * HD) ** -0.5, 0.0625, ((0, 8), (1, 32)))
    return dict(ctx_query=ctx_query, ctx_kv=ctx_kv, new_query=new_query, new_kv=new_kv, out_weight=out_weight)


def stats(queries, keys, values, visible):
    rows = queries.shape[0]
    q = queries.astype(jnp.float32).reshape(rows, GROUP, HD).transpose(1, 0, 2)
    scores = jnp.einsum("grd,kd->grk", q, keys.astype(jnp.float32)) * (HD ** -0.5)
    scores = jnp.where(visible[None], scores, -1e30)
    top = jnp.max(scores, axis=-1)
    weights = jnp.where(visible[None], jnp.exp(scores - top[..., None]), 0.0)
    total = jnp.sum(weights, axis=-1)
    rounded = lax.optimization_barrier(weights.astype(jnp.bfloat16)).astype(jnp.float32)
    summed = jnp.einsum("grk,kd->grd", rounded, values.astype(jnp.float32))
    return top, total, summed


def combine(first, second):
    top = jnp.maximum(first[0], second[0])
    left = jnp.exp(first[0] - top)
    right = jnp.exp(second[0] - top)
    return (top, first[1] * left + second[1] * right,
            first[2] * left[..., None] + second[2] * right[..., None])


def finish(total, summed):
    rows = total.shape[1]
    return (summed / total[..., None]).transpose(1, 0, 2).reshape(rows, GROUP * HD).astype(jnp.bfloat16)


def context_head(queries, keys_all, values_all):
    row = jnp.arange(BLK, dtype=jnp.int32)[:, None]
    col = jnp.arange(2 * BLK, dtype=jnp.int32)[None, :]

    def one_block(item):
        block_rows, index = item
        keys = jnp.concatenate([keys_all[:BLK], lax.dynamic_slice_in_dim(keys_all, index * BLK, BLK, 0)], 0)
        values = jnp.concatenate([values_all[:BLK], lax.dynamic_slice_in_dim(values_all, index * BLK, BLK, 0)], 0)
        visible = jnp.where(col < BLK, index > 0, col - BLK <= row)
        top, total, summed = stats(block_rows, keys, values, visible)
        return finish(total, summed)

    blocks = queries.reshape(N_CTX, BLK, GROUP * HD)
    return lax.map(one_block, (blocks, jnp.arange(N_CTX, dtype=jnp.int32))).reshape(CTX, GROUP * HD)


def query_head(queries, cache_keys, cache_values, fresh_keys, fresh_values):
    row = jnp.arange(QTOK, dtype=jnp.int32)[:, None]
    col = jnp.arange(BLK + QTOK_DEV, dtype=jnp.int32)[None, :]

    def step(carry, index):
        keys = jnp.concatenate([lax.dynamic_slice_in_dim(cache_keys, index * BLK, BLK, 0),
                                lax.dynamic_slice_in_dim(fresh_keys, index * QTOK_DEV, QTOK_DEV, 0)], 0)
        values = jnp.concatenate([lax.dynamic_slice_in_dim(cache_values, index * BLK, BLK, 0),
                                  lax.dynamic_slice_in_dim(fresh_values, index * QTOK_DEV, QTOK_DEV, 0)], 0)
        visible = (col < BLK) | (col - BLK + index * QTOK_DEV <= row)
        return combine(carry, stats(queries, keys, values, visible)), None

    start = (jnp.full((GROUP, QTOK), -1e30, jnp.float32), jnp.zeros((GROUP, QTOK), jnp.float32),
             jnp.zeros((GROUP, QTOK, HD), jnp.float32))
    final, unused = lax.scan(step, start, jnp.arange(N_CTX, dtype=jnp.int32))
    return finish(final[1], final[2])


def reference(ctx_query, ctx_kv, new_query, new_kv, out_weight):
    ctx_out = lax.map(lambda item: context_head(item[0], item[1], item[2]), (ctx_query, ctx_kv[0], ctx_kv[1]))
    attended = lax.map(lambda item: query_head(item[0], item[1], item[2], item[3], item[4]),
                       (new_query, ctx_kv[0], ctx_kv[1], new_kv[0], new_kv[1]))
    attended = attended.transpose(1, 0, 2).reshape(QTOK, KV_HEADS * GROUP * HD)
    new_out = jnp.dot(attended.astype(jnp.float32), out_weight.astype(jnp.float32)).astype(jnp.bfloat16)
    return ctx_out, new_out
```

```python
import math

import jax
import jax.numpy as jnp
from jax import lax
from jax.experimental import pallas as pl
from jax.experimental.pallas import tpu as pltpu
from jax.sharding import PartitionSpec as P

HD = 128
GROUP = 8
BLK = 512
NX, NZ, NY, NC = 4, 8, 4, 2
NCTX, NKV = NX * NZ, NY * NC
QT = 8
ROWS = QT * GROUP
PIECE = BLK // NZ
SCALE = HD**-0.5 * math.log2(math.e)
LOW = -1e30
ZS = (1, 7, 2, 6, 3, 5, 4)
XS = (1, 3, 2)
KVS = ((0, 1), (1, 0), (3, 0), (1, 1), (3, 1), (2, 0), (2, 1))
F32, BF16 = jnp.float32, jnp.bfloat16


def rcopy(src, dst, send, recv, dev):
    return pltpu.make_async_remote_copy(
        src_ref=src,
        dst_ref=dst,
        send_sem=send,
        recv_sem=recv,
        device_id=dev,
        device_id_type=pl.DeviceIdType.MESH,
    )


def scores(q, k):
    return lax.dot_general(q, k, (((1,), (1,)), ((), ())), preferred_element_type=F32) * SCALE


def with_ones(v):
    return jnp.concatenate([v, jnp.ones_like(v)], axis=1)


def weigh(s, top, v1):
    return jnp.dot(jnp.exp2(s - top).astype(BF16), v1, preferred_element_type=F32)


def kernel(
    cq_h, ckv_h, nq_ref, nkv_ref, w_h,
    co_h, no_ref,
    cq, kv, w, fresh, qbuf, anc, own_n, own_m, out, q_n, q_m,
    n_send, n_recv, st_send, st_recv, att, po, po_recv,
    loc, q_ss, q_rs, kv_ss, kv_rs, n_ss, n_rs, an_ss, an_rs, sc_ss, sc_rs,
    az_ss, az_rs, ax_ss, ax_rs, po_ss, po_rs,
):
    here = lax.axis_index("ctx")
    head = lax.axis_index("kv")
    x, z, y, co = here // NZ, here % NZ, head // NC, head % NC

    def zdev(d):
        return (x * NZ + (z + d) % NZ, head)

    def xdev(e):
        return ((x + e) % NX * NZ + z, head)

    def kvdev(dy, dc):
        return (here, (y + dy) % NY * NC + (co + dc) % NC)

    barrier = pltpu.get_barrier_semaphore()
    peers = [zdev(d) for d in ZS] + [xdev(e) for e in XS] + [kvdev(*k) for k in KVS]
    for dev in peers:
        pl.semaphore_signal(barrier, inc=1, device_id=dev, device_id_type=pl.DeviceIdType.MESH)
    load_kv = pltpu.make_async_copy(ckv_h.at[:, 0], kv.at[0], loc.at[0])
    load_cq = pltpu.make_async_copy(cq_h.at[0], cq, loc.at[1])
    load_w = pltpu.make_async_copy(w_h, w, loc.at[2])
    load_kv.start()
    load_cq.start()
    load_w.start()
    nq = nq_ref[0].astype(F32)
    qbuf[0] = jnp.concatenate([nq[:, g * HD : (g + 1) * HD] for g in range(GROUP)], 0).astype(BF16)
    nkv = nkv_ref[:, 0].astype(F32)
    fresh[0] = jnp.concatenate([nkv, jnp.zeros_like(nkv)], 1).astype(BF16)
    pl.semaphore_wait(barrier, len(peers))

    q_copies = {d: rcopy(qbuf.at[0], qbuf.at[d], q_ss.at[d], q_rs.at[d], zdev(d)) for d in ZS}
    for d in ZS:
        q_copies[d].start()
    kv_copies = {}
    for part in range(2):
        for e in XS:
            kv_copies[e, part] = rcopy(
                ckv_h.at[part, 0], kv.at[e, part], kv_ss.at[part, e], kv_rs.at[part, e], xdev(e)
            )
            kv_copies[e, part].start()
        if part == 0:
            for e in XS:
                kv_copies[e, 2] = rcopy(
                    fresh.at[0], fresh.at[e], kv_ss.at[2, e], kv_rs.at[2, e], xdev(e)
                )
                kv_copies[e, 2].start()

    load_kv.wait()
    load_cq.wait()

    def own_head(g, carry):
        cols = pl.ds(pl.multiple_of(g * HD, HD), HD)
        for r in range(4):
            width = (r + 1) * 128
            q = cq[pl.ds(r * 128, 128), cols]
            s = scores(q, kv[0, 0, pl.ds(0, width), :])
            row = lax.broadcasted_iota(jnp.int32, (128, width), 0) + r * 128
            col = lax.broadcasted_iota(jnp.int32, (128, width), 1)
            s = jnp.where(col <= row, s, LOW)
            top = jnp.max(s, axis=1, keepdims=True)
            own_n[g, pl.ds(r * 128, 128), :] = weigh(s, top, with_ones(kv[0, 1, pl.ds(0, width), :]))
            own_m[g, pl.ds(r * 128, 128), :] = jnp.broadcast_to(top, (128, HD))
        return carry

    lax.fori_loop(0, GROUP, own_head, 0)

    for d in ZS:
        q_copies[d].wait_recv()

    def query_block(e):
        def rows(c, carry):
            at = pl.ds(pl.multiple_of(c * 128, 128), 128)
            q = qbuf[pl.ds(c * 2, 2)].reshape(128, HD)
            s = scores(q, kv[e, 0])
            top = jnp.max(s, axis=1, keepdims=True)
            if e == 0:
                q_n[at, :] = weigh(s, top, with_ones(kv[e, 1]))
            else:
                old = q_m[at, :][:, :1]
                top = jnp.maximum(top, old)
                q_n[at, :] = q_n[at, :] * jnp.exp2(old - top) + weigh(s, top, with_ones(kv[e, 1]))
            q_m[at, :] = jnp.broadcast_to(top, (128, HD))
            return carry

        lax.fori_loop(0, NZ * ROWS // 128, rows, 0)

    query_block(0)
    for e in XS:
        kv_copies[e, 0].wait_recv()
        kv_copies[e, 1].wait_recv()
        query_block(e)
    for e in XS:
        kv_copies[e, 2].wait_recv()

    q = qbuf[...].reshape(NZ * ROWS, HD)
    s = scores(q, fresh[:, 0].reshape(NX * 16, HD))
    row = lax.broadcasted_iota(jnp.int32, s.shape, 0)
    col = lax.broadcasted_iota(jnp.int32, s.shape, 1)
    token = (x * NZ + (z - row // ROWS + NZ) % NZ) * QT + row % QT
    key = ((x - col // 16 + NX) % NX * NZ + z) * QT + col % 16
    s = jnp.where((col % 16 < QT) & (key <= token), s, LOW)
    old = q_m[...][:, :1]
    top = jnp.maximum(jnp.max(s, axis=1, keepdims=True), old)
    total = q_n[...] * jnp.exp2(old - top) + weigh(s, top, with_ones(fresh[:, 1].reshape(NX * 16, HD)))
    n_send[...] = (total[:, :HD] / total[:, HD:]).astype(BF16).reshape(NZ, ROWS, HD)
    lse = (top + jnp.log2(total[:, HD:])).reshape(NZ, GROUP, QT, HD)
    lane = lax.broadcasted_iota(jnp.int32, (NZ, QT, HD), 2)
    stat = jnp.full((NZ, QT, HD), 0.0, F32)
    for g in range(GROUP):
        stat = jnp.where(lane == g, lse[:, g], stat)
    st_send[...] = stat

    n_copies = []
    for d in ZS:
        n_copies.append(rcopy(st_send.at[d], st_recv.at[d], n_ss.at[0, d], n_rs.at[0, d], zdev(NZ - d)))
        n_copies.append(rcopy(n_send.at[d], n_recv.at[d], n_ss.at[1, d], n_rs.at[1, d], zdev(NZ - d)))
    for c in n_copies:
        c.start()

    def piece(ref, p):
        return ref.at[:, pl.ds(pl.multiple_of(p * PIECE, PIECE), PIECE)]

    local_anchor = pltpu.make_async_copy(kv.at[x], anc, loc.at[3])
    scatters = [rcopy(piece(kv.at[x], p), piece(anc, p), sc_ss.at[p], sc_rs, zdev(p)) for p in range(1, NZ)]

    @pl.when(z == 0)
    def _():
        for c in scatters:
            c.start()
        local_anchor.start()
        local_anchor.wait()

    @pl.when(z > 0)
    def _():
        rcopy(piece(kv.at[0], 0), piece(anc, z), sc_ss.at[0], sc_rs, zdev(1)).wait_recv()

    spreads = {d: rcopy(piece(anc, z), piece(anc, z), an_ss.at[d], an_rs.at[d], zdev(d)) for d in ZS}
    for d in ZS:

        @pl.when((z + d) % NZ != 0)
        def _():
            spreads[d].start()

    for c in n_copies:
        c.wait_recv()
    st_recv[0] = st_send[0]
    n_recv[0] = n_send[0]
    stats = st_recv[...]
    peak = jnp.max(stats, axis=0)
    share = jnp.exp2(stats - peak[None])
    share = share / jnp.sum(share, axis=0)[None]
    parts = n_recv[...].astype(F32)
    pieces = []
    for g in range(GROUP):
        pieces.append(jnp.sum(parts[:, g * QT : (g + 1) * QT] * share[:, :, g : g + 1], axis=0))
    att[here] = jnp.concatenate(pieces, 0).astype(BF16)

    az = {d: rcopy(att.at[here], att.at[here], az_ss.at[d], az_rs.at[d], zdev(d)) for d in ZS}
    for d in ZS:
        az[d].start()
    ax = {}

    def forward(d):
        block = x * NZ + (z - d + NZ) % NZ
        for e in XS:
            ax[d, e] = rcopy(att.at[block], att.at[block], ax_ss.at[d, e], ax_rs.at[d, e], xdev(e))
            ax[d, e].start()

    forward(0)
    for d in ZS:
        az[d].wait_recv()
        forward(d)

    @pl.when(z > 0)
    def _():
        for d in ZS:
            spreads[d].wait_recv()

    def anchor_head(g, carry):
        cols = pl.ds(pl.multiple_of(g * HD, HD), HD)
        for r in range(4):
            at = pl.ds(r * 128, 128)
            s = scores(cq[at, cols], anc[0])
            top = jnp.max(s, axis=1, keepdims=True)
            n = weigh(s, top, with_ones(anc[1]))
            old = own_m[g, at, :]
            peak = jnp.maximum(old, top)
            mine = jnp.where(here > 0, jnp.exp2(old - peak), 1.0)
            theirs = jnp.where(here > 0, jnp.exp2(top - peak), 0.0)
            summed = own_n[g, at, :]
            total = summed[:, HD:] * mine + n[:, HD:] * theirs
            out[at, cols] = ((summed[:, :HD] * mine + n[:, :HD] * theirs) / total).astype(BF16)
        return carry

    lax.fori_loop(0, GROUP, anchor_head, 0)
    store_out = pltpu.make_async_copy(out, co_h.at[0], loc.at[4])
    store_out.start()

    load_w.wait()
    for c in ax.values():
        c.wait_recv()
    acc = jnp.zeros((NCTX * QT, no_ref.shape[1]), F32)
    for j in range(GROUP // 2):
        pair = att[:, pl.ds(j * 16, 16), :].astype(F32)
        lhs = jnp.concatenate(
            [pair[:, :QT].reshape(NCTX * QT, HD), pair[:, QT:].reshape(NCTX * QT, HD)], 1
        ).astype(BF16)
        acc = acc + jnp.dot(lhs, w[pl.ds(j * 256, 256), :], preferred_element_type=F32)
    po[...] = acc.reshape(po.shape)
    po_copies = []
    for i, (dy, dc) in enumerate(KVS):
        dest = (y + dy) % NY * NC + (co + dc) % NC
        po_copies.append(rcopy(po.at[dest], po_recv.at[i], po_ss.at[i], po_rs.at[i], (here, dest)))
        po_copies[i].start()
    total = po[head]
    for i, c in enumerate(po_copies):
        c.wait_recv()
        total = total + po_recv[i]
    no_ref[...] = total.astype(BF16)

    for group in (q_copies, kv_copies, az, ax):
        for c in group.values():
            c.wait_send()
    for c in n_copies + po_copies:
        c.wait_send()
    for d in ZS:

        @pl.when((z + d) % NZ != 0)
        def _():
            spreads[d].wait_send()

    @pl.when(z == 0)
    def _():
        for c in scatters:
            c.wait_send()

    store_out.wait()


def body(ctx_query, ctx_kv, new_query, new_kv, out_weight):
    any_space = pl.BlockSpec(memory_space=pl.ANY)
    vmem = pl.BlockSpec(memory_space=pltpu.VMEM)
    cols = out_weight.shape[1]
    mine = NCTX * QT // NKV
    dma = pltpu.SemaphoreType.DMA
    return pl.pallas_call(
        kernel,
        out_shape=(
            jax.ShapeDtypeStruct(ctx_query.shape, BF16),
            jax.ShapeDtypeStruct((mine, cols), BF16),
        ),
        in_specs=[any_space, any_space, vmem, vmem, any_space],
        out_specs=(any_space, vmem),
        scratch_shapes=[
            pltpu.VMEM((BLK, GROUP * HD), BF16),
            pltpu.VMEM((NX, 2, BLK, HD), BF16),
            pltpu.VMEM((GROUP * HD, cols), BF16),
            pltpu.VMEM((NX, 2, 16, HD), BF16),
            pltpu.VMEM((NZ, ROWS, HD), BF16),
            pltpu.VMEM((2, BLK, HD), BF16),
            pltpu.VMEM((GROUP, BLK, 2 * HD), F32),
            pltpu.VMEM((GROUP, BLK, HD), F32),
            pltpu.VMEM((BLK, GROUP * HD), BF16),
            pltpu.VMEM((NZ * ROWS, 2 * HD), F32),
            pltpu.VMEM((NZ * ROWS, HD), F32),
            pltpu.VMEM((NZ, ROWS, HD), BF16),
            pltpu.VMEM((NZ, ROWS, HD), BF16),
            pltpu.VMEM((NZ, QT, HD), F32),
            pltpu.VMEM((NZ, QT, HD), F32),
            pltpu.VMEM((NCTX, ROWS, HD), BF16),
            pltpu.VMEM((NKV, mine, cols), F32),
            pltpu.VMEM((NKV - 1, mine, cols), F32),
            dma((5,)),
            dma((NZ,)), dma((NZ,)),
            dma((3, NX)), dma((3, NX)),
            dma((2, NZ)), dma((2, NZ)),
            dma((NZ,)), dma((NZ,)),
            dma((NZ,)), dma,
            dma((NZ,)), dma((NZ,)),
            dma((NZ, NX)), dma((NZ, NX)),
            dma((NKV,)), dma((NKV,)),
        ],
        compiler_params=pltpu.CompilerParams(
            collective_id=0, has_side_effects=True, vmem_limit_bytes=40 * 1024 * 1024
        ),
        name="star",
    )(ctx_query, ctx_kv, new_query, new_kv, out_weight)


def solution(mesh):
    return jax.shard_map(
        body,
        mesh=mesh,
        in_specs=(
            P("kv", "ctx", None),
            P(None, "kv", "ctx", None),
            P("kv", "ctx", None),
            P(None, "kv", "ctx", None),
            P("kv", "ctx"),
        ),
        out_specs=(P("kv", "ctx", None), P("kv", "ctx")),
        check_vma=False,
    )
```

```python
import math

import jax
import jax.numpy as jnp
from jax import lax
from jax.experimental import pallas as pl
from jax.experimental.pallas import tpu as pltpu
from jax.sharding import PartitionSpec as P

HD = 128
GROUP = 8
BLK = 512
NX, NZ, NY, NC = 4, 8, 4, 2
NCTX, NKV = NX * NZ, NY * NC
QT = 8
ROWS = QT * GROUP
PIECE = BLK // NZ
SCALE = HD**-0.5 * math.log2(math.e)
LOW = -1e30
ZS = (1, 7, 2, 6, 3, 5, 4)
XS = (1, 3, 2)
KVS = ((0, 1), (1, 0), (3, 0), (1, 1), (3, 1), (2, 0), (2, 1))
F32, BF16 = jnp.float32, jnp.bfloat16


def rcopy(src, dst, send, recv, dev):
    return pltpu.make_async_remote_copy(
        src_ref=src,
        dst_ref=dst,
        send_sem=send,
        recv_sem=recv,
        device_id=dev,
        device_id_type=pl.DeviceIdType.MESH,
    )


def scores(q, k):
    return lax.dot_general(q, k, (((1,), (1,)), ((), ())), preferred_element_type=F32)


def with_ones(v):
    return jnp.concatenate([v, jnp.ones_like(v)], axis=1)


def weigh(s, top, v1):
    return jnp.dot(jnp.exp2((s - top) * SCALE).astype(BF16), v1, preferred_element_type=F32)


def peak_of(s):
    return jnp.max(s, axis=1, keepdims=True)


def kernel(
    cq_h, ckv_h, nq_ref, nkv_ref, w_h,
    co_h, no_ref,
    cq, kv, w, fresh, qbuf, anc, own_n, own_m, out, q_n, q_m,
    n_send, n_recv, st_send, st_recv, att, po, po_recv,
    loc, q_ss, q_rs, kv_ss, kv_rs, n_ss, n_rs, an_ss, an_rs, sc_ss, sc_rs,
    az_ss, az_rs, ax_ss, ax_rs, po_ss, po_rs,
):
    here = lax.axis_index("ctx")
    head = lax.axis_index("kv")
    x, z, y, co = here // NZ, here % NZ, head // NC, head % NC

    def zdev(d):
        return (x * NZ + (z + d) % NZ, head)

    def xdev(e):
        return ((x + e) % NX * NZ + z, head)

    def kvdev(dy, dc):
        return (here, (y + dy) % NY * NC + (co + dc) % NC)

    barrier = pltpu.get_barrier_semaphore()
    peers = [zdev(d) for d in ZS] + [xdev(e) for e in XS] + [kvdev(*k) for k in KVS]
    for dev in peers:
        pl.semaphore_signal(barrier, inc=1, device_id=dev, device_id_type=pl.DeviceIdType.MESH)
    load_kv = pltpu.make_async_copy(ckv_h.at[:, 0], kv.at[0], loc.at[0])
    load_cq = pltpu.make_async_copy(cq_h.at[0], cq, loc.at[1])
    load_w = pltpu.make_async_copy(w_h, w, loc.at[2])
    load_kv.start()
    load_cq.start()
    load_w.start()
    nq = nq_ref[0].astype(F32)
    qbuf[0] = jnp.concatenate([nq[:, g * HD : (g + 1) * HD] for g in range(GROUP)], 0).astype(BF16)
    nkv = nkv_ref[:, 0].astype(F32)
    fresh[0] = jnp.concatenate([nkv, jnp.zeros_like(nkv)], 1).astype(BF16)
    pl.semaphore_wait(barrier, len(peers))

    q_copies = {d: rcopy(qbuf.at[0], qbuf.at[d], q_ss.at[d], q_rs.at[d], zdev(d)) for d in ZS}
    for d in ZS:
        q_copies[d].start()
    kv_copies = {}

    def send_kv(name, src, dst, dev):
        kv_copies[name] = rcopy(src, dst, kv_ss.at[len(kv_copies)], kv_rs.at[len(kv_copies)], dev)
        kv_copies[name].start()

    for e in XS:
        send_kv(("fresh", e), fresh.at[0], fresh.at[e], xdev(e))
    for part in range(2):
        for e in (1, 3):
            send_kv((part, e), ckv_h.at[part, 0], kv.at[e, part], xdev(e))

    def pass_on(part):
        for e in (1, 3):
            half = pl.ds((e // 2) * (BLK // 2), BLK // 2)
            kv_copies[part, e].wait_recv()
            send_kv((part, 2, e), kv.at[e, part, half], kv.at[2, part, half], xdev(e))

    load_kv.wait()
    load_cq.wait()

    keep = lax.broadcasted_iota(jnp.int32, (128, 128), 1) <= lax.broadcasted_iota(
        jnp.int32, (128, 128), 0
    )

    def own_head(g, carry):
        cols = pl.ds(pl.multiple_of(g * HD, HD), HD)
        tiles = [pl.ds(r * 128, 128) for r in range(4)]
        found = [
            scores(cq[at, cols], kv[0, 0, pl.ds(0, (r + 1) * 128), :]) for r, at in enumerate(tiles)
        ]
        weights = []
        for r, at in enumerate(tiles):
            s = jnp.where(keep, found[r][:, r * 128 :], LOW)
            if r:
                s = jnp.concatenate([found[r][:, : r * 128], s], 1)
            top = peak_of(s)
            weights.append(jnp.exp2((s - top) * SCALE).astype(BF16))
            own_m[g, at, :] = jnp.broadcast_to(top, (128, HD))
        for r, at in enumerate(tiles):
            v1 = with_ones(kv[0, 1, pl.ds(0, (r + 1) * 128), :])
            own_n[g, at, :] = jnp.dot(weights[r], v1, preferred_element_type=F32)
        return carry

    lax.fori_loop(0, GROUP, own_head, 0, unroll=4)

    pass_on(0)
    for d in ZS:
        q_copies[d].wait_recv()
    for e in XS:
        kv_copies["fresh", e].wait_recv()

    row = lax.broadcasted_iota(jnp.int32, (128, NX * 16), 0)
    col = lax.broadcasted_iota(jnp.int32, (128, NX * 16), 1)
    key = ((x - col // 16 + NX) % NX * NZ + z) * QT + col % 16
    chunks = range(NZ * ROWS // 128)
    rows = [pl.ds(c * 128, 128) for c in chunks]
    qs = [qbuf[pl.ds(c * 2, 2)].reshape(128, HD) for c in chunks]
    fresh_k = fresh[:, 0].reshape(NX * 16, HD)
    fresh_v = with_ones(fresh[:, 1].reshape(NX * 16, HD))
    found = [(scores(q, fresh_k), scores(q, kv[0, 0])) for q in qs]
    tops = []
    for c in chunks:
        token = (x * NZ + (z - c * 2 - row // ROWS + NZ) % NZ) * QT + row % QT
        s = jnp.where((col % 16 < QT) & (key <= token), found[c][0], LOW)
        top = jnp.maximum(peak_of(s), peak_of(found[c][1]))
        q_n[rows[c], :] = weigh(s, top, fresh_v) + weigh(found[c][1], top, with_ones(kv[0, 1]))
        q_m[rows[c], :] = jnp.broadcast_to(top, (128, HD))

    pass_on(1)
    found = [(scores(q, kv[1, 0]), scores(q, kv[3, 0])) for q in qs]
    for c in chunks:
        old = q_m[rows[c], :][:, :1]
        top = jnp.maximum(jnp.maximum(old, peak_of(found[c][0])), peak_of(found[c][1]))
        fade = jnp.exp2((old - top) * SCALE)
        q_n[rows[c], :] = (
            q_n[rows[c], :] * fade
            + weigh(found[c][0], top, with_ones(kv[1, 1]))
            + weigh(found[c][1], top, with_ones(kv[3, 1]))
        )
        q_m[rows[c], :] = jnp.broadcast_to(top, (128, HD))

    for part in range(2):
        for e in (1, 3):
            kv_copies[part, 2, e].wait_recv()
    found = [scores(q, kv[2, 0]) for q in qs]
    totals, lses = [], []
    for c in chunks:
        old = q_m[rows[c], :][:, :1]
        top = jnp.maximum(old, peak_of(found[c]))
        n = q_n[rows[c], :] * jnp.exp2((old - top) * SCALE) + weigh(found[c], top, with_ones(kv[2, 1]))
        totals.append(n[:, :HD] / n[:, HD:])
        lses.append(top * SCALE + jnp.log2(n[:, HD:]))
    lse = jnp.concatenate(lses, 0).reshape(NZ, GROUP, QT, HD)
    n_send[...] = jnp.concatenate(totals, 0).astype(BF16).reshape(NZ, ROWS, HD)
    lane = lax.broadcasted_iota(jnp.int32, (NZ, QT, HD), 2)
    stat = jnp.full((NZ, QT, HD), 0.0, F32)
    for g in range(GROUP):
        stat = jnp.where(lane == g, lse[:, g], stat)
    st_send[...] = stat

    n_copies = []
    for d in ZS:
        n_copies.append(rcopy(st_send.at[d], st_recv.at[d], n_ss.at[0, d], n_rs.at[0, d], zdev(NZ - d)))
        n_copies.append(rcopy(n_send.at[d], n_recv.at[d], n_ss.at[1, d], n_rs.at[1, d], zdev(NZ - d)))
    for c in n_copies:
        c.start()

    def piece(ref, p):
        return ref.at[:, pl.ds(pl.multiple_of(p * PIECE, PIECE), PIECE)]

    local_anchor = pltpu.make_async_copy(kv.at[x], anc, loc.at[3])
    scatters = [rcopy(piece(kv.at[x], p), piece(anc, p), sc_ss.at[p], sc_rs, zdev(p)) for p in range(1, NZ)]

    @pl.when(z == 0)
    def _():
        for c in scatters:
            c.start()
        local_anchor.start()
        local_anchor.wait()

    @pl.when(z > 0)
    def _():
        rcopy(piece(kv.at[0], 0), piece(anc, z), sc_ss.at[0], sc_rs, zdev(1)).wait_recv()

    for c in n_copies:
        c.wait_recv()
    st_recv[0] = st_send[0]
    n_recv[0] = n_send[0]
    stats = st_recv[...]
    peak = jnp.max(stats, axis=0)
    share = jnp.exp2(stats - peak[None])
    share = share / jnp.sum(share, axis=0)[None]
    parts = n_recv[...].astype(F32)
    pieces = []
    for g in range(GROUP):
        pieces.append(jnp.sum(parts[:, g * QT : (g + 1) * QT] * share[:, :, g : g + 1], axis=0))
    att[here] = jnp.concatenate(pieces, 0).astype(BF16)

    az = {d: rcopy(att.at[here], att.at[here], az_ss.at[d], az_rs.at[d], zdev(d)) for d in ZS}
    for d in ZS:
        az[d].start()
    ax = {}

    def forward(d):
        block = x * NZ + (z - d + NZ) % NZ
        for e in XS:
            ax[d, e] = rcopy(att.at[block], att.at[block], ax_ss.at[d, e], ax_rs.at[d, e], xdev(e))
            ax[d, e].start()

    forward(0)
    spreads = {d: rcopy(piece(anc, z), piece(anc, z), an_ss.at[d], an_rs.at[d], zdev(d)) for d in ZS}
    for d in ZS:

        @pl.when((z + d) % NZ != 0)
        def _():
            spreads[d].start()

    for d in ZS:
        az[d].wait_recv()
        forward(d)

    load_w.wait()
    mine = NCTX * QT // NKV
    po_copies = {}

    def project(e):
        block = (x - e + NX) % NX
        lhs = att[pl.ds(block * NZ, NZ)].astype(F32)
        acc = jnp.zeros((NZ * QT, no_ref.shape[1]), F32)
        for j in range(GROUP // 2):
            pair = [lhs[:, g * QT : (g + 1) * QT].reshape(NZ * QT, HD) for g in (2 * j, 2 * j + 1)]
            acc = acc + jnp.dot(
                jnp.concatenate(pair, 1).astype(BF16),
                w[pl.ds(j * 2 * HD, 2 * HD), :],
                preferred_element_type=F32,
            )
        po[pl.ds(block * NC, NC)] = acc.reshape(NC, mine, acc.shape[1])
        for c in range(NC):
            dest = block * NC + c
            po_copies[e, c] = rcopy(
                po.at[dest], po_recv.at[head], po_ss.at[e * NC + c], po_rs.at[head], (here, dest)
            )

            @pl.when(dest != head)
            def _():
                po_copies[e, c].start()

    project(0)
    for e in XS:
        for d in (0,) + ZS:
            ax[d, e].wait_recv()
        project(e)

    @pl.when(z > 0)
    def _():
        for d in ZS:
            spreads[d].wait_recv()

    def anchor_head(g, carry):
        cols = pl.ds(pl.multiple_of(g * HD, HD), HD)
        for r in range(4):
            at = pl.ds(r * 128, 128)
            s = scores(cq[at, cols], anc[0])
            top = peak_of(s)
            n = weigh(s, top, with_ones(anc[1]))
            old = own_m[g, at, :]
            peak = jnp.maximum(old, top)
            mine = jnp.where(here > 0, jnp.exp2((old - peak) * SCALE), 1.0)
            theirs = jnp.where(here > 0, jnp.exp2((top - peak) * SCALE), 0.0)
            summed = own_n[g, at, :]
            total = summed[:, HD:] * mine + n[:, HD:] * theirs
            out[at, cols] = ((summed[:, :HD] * mine + n[:, :HD] * theirs) / total).astype(BF16)
        return carry

    lax.fori_loop(0, GROUP, anchor_head, 0, unroll=4)
    store_out = pltpu.make_async_copy(out, co_h.at[0], loc.at[4])
    store_out.start()

    total = po[head]
    for dy, dc in KVS:
        source = (y + dy) % NY * NC + (co + dc) % NC
        rcopy(po.at[0], po_recv.at[source], po_ss.at[0], po_rs.at[source], (here, source)).wait_recv()
        total = total + po_recv[source]
    no_ref[...] = total.astype(BF16)

    for group in (q_copies, kv_copies, az, ax):
        for c in group.values():
            c.wait_send()
    for c in n_copies:
        c.wait_send()
    for e in range(NX):
        for c in range(NC):

            @pl.when((x - e + NX) % NX * NC + c != head)
            def _():
                po_copies[e, c].wait_send()

    for d in ZS:

        @pl.when((z + d) % NZ != 0)
        def _():
            spreads[d].wait_send()

    @pl.when(z == 0)
    def _():
        for c in scatters:
            c.wait_send()

    store_out.wait()


def body(ctx_query, ctx_kv, new_query, new_kv, out_weight):
    any_space = pl.BlockSpec(memory_space=pltpu.HBM)
    vmem = pl.BlockSpec(memory_space=pltpu.VMEM)
    cols = out_weight.shape[1]
    mine = NCTX * QT // NKV
    dma = pltpu.SemaphoreType.DMA
    return pl.pallas_call(
        kernel,
        out_shape=(
            jax.ShapeDtypeStruct(ctx_query.shape, BF16),
            jax.ShapeDtypeStruct((mine, cols), BF16),
        ),
        in_specs=[any_space, any_space, vmem, vmem, any_space],
        out_specs=(any_space, vmem),
        scratch_shapes=[
            pltpu.VMEM((BLK, GROUP * HD), BF16),
            pltpu.VMEM((NX, 2, BLK, HD), BF16),
            pltpu.VMEM((GROUP * HD, cols), BF16),
            pltpu.VMEM((NX, 2, 16, HD), BF16),
            pltpu.VMEM((NZ, ROWS, HD), BF16),
            pltpu.VMEM((2, BLK, HD), BF16),
            pltpu.VMEM((GROUP, BLK, 2 * HD), F32),
            pltpu.VMEM((GROUP, BLK, HD), F32),
            pltpu.VMEM((BLK, GROUP * HD), BF16),
            pltpu.VMEM((NZ * ROWS, 2 * HD), F32),
            pltpu.VMEM((NZ * ROWS, HD), F32),
            pltpu.VMEM((NZ, ROWS, HD), BF16),
            pltpu.VMEM((NZ, ROWS, HD), BF16),
            pltpu.VMEM((NZ, QT, HD), F32),
            pltpu.VMEM((NZ, QT, HD), F32),
            pltpu.VMEM((NCTX, ROWS, HD), BF16),
            pltpu.VMEM((NKV, mine, cols), F32),
            pltpu.VMEM((NKV, mine, cols), F32),
            dma((5,)),
            dma((NZ,)), dma((NZ,)),
            dma((11,)), dma((11,)),
            dma((2, NZ)), dma((2, NZ)),
            dma((NZ,)), dma((NZ,)),
            dma((NZ,)), dma,
            dma((NZ,)), dma((NZ,)),
            dma((NZ, NX)), dma((NZ, NX)),
            dma((NKV,)), dma((NKV,)),
        ],
        compiler_params=pltpu.CompilerParams(
            collective_id=0, has_side_effects=True, vmem_limit_bytes=60 * 1024 * 1024
        ),
        name="star",
    )(ctx_query, ctx_kv, new_query, new_kv, out_weight)


def solution(mesh):
    return jax.shard_map(
        body,
        mesh=mesh,
        in_specs=(
            P("kv", "ctx", None),
            P(None, "kv", "ctx", None),
            P("kv", "ctx", None),
            P(None, "kv", "ctx", None),
            P("kv", "ctx"),
        ),
        out_specs=(P("kv", "ctx", None), P("kv", "ctx")),
        check_vma=False,
    )
```

```python
import math

import jax
import jax.numpy as jnp
from jax import lax
from jax.experimental import pallas as pl
from jax.experimental.pallas import tpu as pltpu
from jax.sharding import PartitionSpec as P

HD = 128
GROUP = 8
BLK = 512
NX, NZ, NY, NC = 4, 8, 4, 2
NCTX, NKV = NX * NZ, NY * NC
QT = 8
ROWS = QT * GROUP
STRIPE = BLK // NX
PIECE = STRIPE // NZ
SCALE = HD**-0.5 * math.log2(math.e)
LOW = -1e30
ZS = (1, 7, 2, 6, 3, 5, 4)
FAR = ZS[::-1]
SIDES = (1, 3, 2)
KVS = ((0, 1), (1, 0), (3, 0), (1, 1), (3, 1), (2, 0), (2, 1))
F32, BF16 = jnp.float32, jnp.bfloat16


def rcopy(src, dst, send, recv, dev):
    return pltpu.make_async_remote_copy(
        src_ref=src,
        dst_ref=dst,
        send_sem=send,
        recv_sem=recv,
        device_id=dev,
        device_id_type=pl.DeviceIdType.MESH,
    )


def scores(q, k):
    return lax.dot_general(q, k, (((1,), (1,)), ((), ())), preferred_element_type=F32)


def with_ones(v):
    return jnp.concatenate([v, jnp.ones_like(v)], axis=1)


def weigh(s, top, v1):
    return jnp.dot(jnp.exp2((s - top) * SCALE).astype(BF16), v1, preferred_element_type=F32)


def peak_of(s):
    return jnp.max(s, axis=1, keepdims=True)


def kernel(
    cq_h, ckv_h, nq_ref, nkv_ref, w_h,
    co_h, no_ref,
    cq, kv, w, fresh, qbuf, anc, own_n, own_m, out, q_n, q_m,
    n_send, n_recv, st_send, st_recv, att, po, po_recv,
    loc, q_ss, q_rs, kv_ss, kv_rs, n_ss, n_rs, an_ss, an_rs, sc_ss, sc_rs, pass_ss, pass_rs, st_ss, st_rs,
    az_ss, az_rs, ax_ss, ax_rs, po_ss, po_rs,
):
    here = lax.axis_index("ctx")
    head = lax.axis_index("kv")
    x, z, y, co = here // NZ, here % NZ, head // NC, head % NC

    def member(d):
        return (x + 2 * (d % 2)) % NX * NZ + (z + d) % NZ

    colour = (x + 2 * (z % 2)) % NX

    def zdev(d):
        return (member(d), head)

    def side(e):
        if e % 2:
            return ((x + e) % NX * NZ + z, head)
        return (x * NZ + (z + (1 if e == 2 else NZ - 1)) % NZ, head)

    def kvdev(dy, dc):
        return (here, (y + dy) % NY * NC + (co + dc) % NC)

    barrier = pltpu.get_barrier_semaphore()
    peers = [zdev(d) for d in ZS] + [side(e) for e in (1, 3, 2, 4)] + [kvdev(*k) for k in KVS]
    for dev in peers:
        pl.semaphore_signal(barrier, inc=1, device_id=dev, device_id_type=pl.DeviceIdType.MESH)
    load_kv = pltpu.make_async_copy(ckv_h.at[:, 0], kv.at[0], loc.at[0])
    load_cq = pltpu.make_async_copy(cq_h.at[0], cq, loc.at[1])
    load_w = pltpu.make_async_copy(w_h, w, loc.at[2])
    load_kv.start()
    load_cq.start()
    load_w.start()
    nq = nq_ref[0].astype(F32)
    qbuf[0] = jnp.concatenate([nq[:, g * HD : (g + 1) * HD] for g in range(GROUP)], 0).astype(BF16)
    nkv = nkv_ref[:, 0].astype(F32)
    fresh[0] = jnp.concatenate([nkv, jnp.zeros_like(nkv)], 1).astype(BF16)
    pl.semaphore_wait(barrier, len(peers))

    q_copies = {d: rcopy(qbuf.at[0], qbuf.at[d], q_ss.at[d], q_rs.at[d], zdev(d)) for d in ZS}
    for d in FAR:
        q_copies[d].start()
    kv_copies = {}

    def send_kv(name, src, dst, dev):
        kv_copies[name] = rcopy(src, dst, kv_ss.at[len(kv_copies)], kv_rs.at[len(kv_copies)], dev)
        kv_copies[name].start()

    for e in SIDES:
        send_kv(("fresh", e), fresh.at[0], fresh.at[e], side(e))
    for part in range(2):
        for e in (1, 3):
            send_kv((part, e), ckv_h.at[part, 0], kv.at[e, part], side(e))
        for e in (2, 4):
            half = pl.ds((e // 2 - 1) * (BLK // 2), BLK // 2)
            send_kv((part, e), ckv_h.at[part, 0, half], kv.at[2, part, half], side(e))

    load_kv.wait()
    load_cq.wait()

    keep = lax.broadcasted_iota(jnp.int32, (128, 128), 1) <= lax.broadcasted_iota(
        jnp.int32, (128, 128), 0
    )

    def own_head(g, carry):
        cols = pl.ds(pl.multiple_of(g * HD, HD), HD)
        tiles = [pl.ds(r * 128, 128) for r in range(4)]
        found = [
            scores(cq[at, cols], kv[0, 0, pl.ds(0, (r + 1) * 128), :]) for r, at in enumerate(tiles)
        ]
        weights = []
        for r, at in enumerate(tiles):
            s = jnp.where(keep, found[r][:, r * 128 :], LOW)
            if r:
                s = jnp.concatenate([found[r][:, : r * 128], s], 1)
            top = peak_of(s)
            weights.append(jnp.exp2((s - top) * SCALE).astype(BF16))
            own_m[g, at, :] = jnp.broadcast_to(top, (128, HD))
        for r, at in enumerate(tiles):
            v1 = with_ones(kv[0, 1, pl.ds(0, (r + 1) * 128), :])
            own_n[g, at, :] = jnp.dot(weights[r], v1, preferred_element_type=F32)
        return carry

    lax.fori_loop(0, GROUP, own_head, 0, unroll=4)

    for d in ZS:
        q_copies[d].wait_recv()
    for e in SIDES:
        kv_copies["fresh", e].wait_recv()
    for part in range(2):
        for e in (2, 4):
            kv_copies[part, e].wait_recv()

    row = lax.broadcasted_iota(jnp.int32, (128, NX * 16), 0)
    col = lax.broadcasted_iota(jnp.int32, (128, NX * 16), 1)
    slot = col // 16
    key_x = jnp.where(slot == 2, x, (x - slot + NX) % NX)
    key_z = jnp.where(slot == 2, (z + NZ - 1) % NZ, z)
    key = (key_x * NZ + key_z) * QT + col % 16
    chunks = range(NZ * ROWS // 128)
    rows = [pl.ds(c * 128, 128) for c in chunks]
    qs = [qbuf[pl.ds(c * 2, 2)].reshape(128, HD) for c in chunks]
    fresh_k = fresh[:, 0].reshape(NX * 16, HD)
    fresh_v = with_ones(fresh[:, 1].reshape(NX * 16, HD))
    found = [(scores(q, fresh_k), scores(q, kv[0, 0]), scores(q, kv[2, 0])) for q in qs]
    for c in chunks:
        came = c * 2 + row // ROWS
        token = ((x + 2 * (came % 2)) % NX * NZ + (z - came + NZ) % NZ) * QT + row % QT
        s = jnp.where((col % 16 < QT) & (key <= token), found[c][0], LOW)
        top = jnp.maximum(jnp.maximum(peak_of(s), peak_of(found[c][1])), peak_of(found[c][2]))
        q_n[rows[c], :] = (
            weigh(s, top, fresh_v)
            + weigh(found[c][1], top, with_ones(kv[0, 1]))
            + weigh(found[c][2], top, with_ones(kv[2, 1]))
        )
        q_m[rows[c], :] = jnp.broadcast_to(top, (128, HD))

    for part in range(2):
        for e in (1, 3):
            kv_copies[part, e].wait_recv()

    def stripe(ref, k):
        return ref.at[:, pl.ds(pl.multiple_of(k * STRIPE, STRIPE), STRIPE)]

    def piece(p):
        return anc.at[:, pl.ds(pl.multiple_of(colour * STRIPE + p * PIECE, PIECE), PIECE)]

    local_stripe = pltpu.make_async_copy(stripe(kv.at[x], x), stripe(anc, x), loc.at[3])
    far_stripe = rcopy(stripe(kv.at[1], 2), stripe(anc, 2), pass_ss, pass_rs, side(1))

    @pl.when((z == 0) & (x != 2))
    def _():
        local_stripe.start()

    @pl.when(here == NZ)
    def _():
        far_stripe.start()

    found = [(scores(q, kv[1, 0]), scores(q, kv[3, 0])) for q in qs]
    totals, lses = [], []
    for c in chunks:
        old = q_m[rows[c], :][:, :1]
        top = jnp.maximum(jnp.maximum(old, peak_of(found[c][0])), peak_of(found[c][1]))
        n = (
            q_n[rows[c], :] * jnp.exp2((old - top) * SCALE)
            + weigh(found[c][0], top, with_ones(kv[1, 1]))
            + weigh(found[c][1], top, with_ones(kv[3, 1]))
        )
        totals.append(n[:, :HD] / n[:, HD:])
        lses.append(top * SCALE + jnp.log2(n[:, HD:]))
    lse = jnp.concatenate(lses, 0).reshape(NZ, GROUP, QT, HD)
    n_send[...] = jnp.concatenate(totals, 0).astype(BF16).reshape(NZ, ROWS, HD)
    lane = lax.broadcasted_iota(jnp.int32, (NZ, QT, HD), 2)
    stat = jnp.full((NZ, QT, HD), 0.0, F32)
    for g in range(GROUP):
        stat = jnp.where(lane == g, lse[:, g], stat)
    st_send[...] = stat

    n_copies = []
    for d in FAR:
        n_copies.append(rcopy(st_send.at[d], st_recv.at[d], n_ss.at[0, d], n_rs.at[0, d], zdev(NZ - d)))
        n_copies.append(rcopy(n_send.at[d], n_recv.at[d], n_ss.at[1, d], n_rs.at[1, d], zdev(NZ - d)))
    for c in n_copies:
        c.start()

    scatters = [rcopy(piece(p), piece(p), sc_ss.at[p], sc_rs, zdev(p)) for p in range(1, NZ)]

    @pl.when((z == 0) & (x != 2))
    def _():
        local_stripe.wait()

    @pl.when(here == 2 * NZ)
    def _():
        far_stripe.wait_recv()

    @pl.when(z == 0)
    def _():
        for c in scatters:
            c.start()

    for c in n_copies:
        c.wait_recv()
    st_recv[0] = st_send[0]
    n_recv[0] = n_send[0]
    stats = st_recv[...]
    peak = jnp.max(stats, axis=0)
    share = jnp.exp2(stats - peak[None])
    share = share / jnp.sum(share, axis=0)[None]
    parts = n_recv[...].astype(F32)
    pieces = []
    for g in range(GROUP):
        pieces.append(jnp.sum(parts[:, g * QT : (g + 1) * QT] * share[:, :, g : g + 1], axis=0))
    att[here] = jnp.concatenate(pieces, 0).astype(BF16)

    az = {d: rcopy(att.at[here], att.at[here], az_ss.at[d], az_rs.at[d], zdev(d)) for d in ZS}
    for d in FAR:
        az[d].start()
    ax = {}

    def forward(d):
        block = member(NZ - d)
        for e in SIDES:
            dev = side(4) if e == 2 and d % 2 else side(e)
            ax[d, e] = rcopy(att.at[block], att.at[block], ax_ss.at[d, e], ax_rs.at[d, e], dev)
            ax[d, e].start()

    forward(0)

    @pl.when(z > 0)
    def _():
        rcopy(piece(0), piece(z), sc_ss.at[0], sc_rs, zdev(1)).wait_recv()

    spreads = {d: rcopy(piece(z), piece(z), an_ss.at[d], an_rs.at[d], zdev(d)) for d in ZS}
    for d in FAR:

        @pl.when((z + d) % NZ != 0)
        def _():
            spreads[d].start()

    for d in ZS:
        az[d].wait_recv()
        forward(d)

    @pl.when(z > 0)
    def _():
        for d in ZS:
            spreads[d].wait_recv()

    stripes = []
    for e in (1, 3):
        mine = stripe(anc, colour)
        stripes.append(rcopy(mine, mine, st_ss.at[e], st_rs.at[e], side(e)))
    for e in (2, 4):
        first = colour * STRIPE + (e // 2 - 1) * (STRIPE // 2)
        mine = anc.at[:, pl.ds(pl.multiple_of(first, STRIPE // 2), STRIPE // 2)]
        stripes.append(rcopy(mine, mine, st_ss.at[e], st_rs.at[e], side(e)))
    for c in stripes:
        c.start()

    load_w.wait()
    mine = NCTX * QT // NKV
    po_copies = {}

    def project(e):
        block = (x - e + NX) % NX
        lhs = att[pl.ds(block * NZ, NZ)].astype(F32)
        acc = jnp.zeros((NZ * QT, no_ref.shape[1]), F32)
        for j in range(GROUP // 2):
            pair = [lhs[:, g * QT : (g + 1) * QT].reshape(NZ * QT, HD) for g in (2 * j, 2 * j + 1)]
            acc = acc + jnp.dot(
                jnp.concatenate(pair, 1).astype(BF16),
                w[pl.ds(j * 2 * HD, 2 * HD), :],
                preferred_element_type=F32,
            )
        po[pl.ds(block * NC, NC)] = acc.reshape(NC, mine, acc.shape[1])
        for c in range(NC):
            dest = block * NC + c
            po_copies[e, c] = rcopy(
                po.at[dest], po_recv.at[head], po_ss.at[e * NC + c], po_rs.at[head], (here, dest)
            )

            @pl.when(dest != head)
            def _():
                po_copies[e, c].start()

    for d in (0,) + ZS:
        ax[d, 2].wait_recv()
    project(0)
    project(2)
    for d in (0,) + ZS:
        ax[d, 1].wait_recv()
        ax[d, 3].wait_recv()
    project(1)
    project(3)

    for c in stripes:
        c.wait_recv()

    def anchor_head(g, carry):
        cols = pl.ds(pl.multiple_of(g * HD, HD), HD)
        for r in range(4):
            at = pl.ds(r * 128, 128)
            s = scores(cq[at, cols], anc[0])
            top = peak_of(s)
            n = weigh(s, top, with_ones(anc[1]))
            old = own_m[g, at, :]
            peak = jnp.maximum(old, top)
            mine = jnp.where(here > 0, jnp.exp2((old - peak) * SCALE), 1.0)
            theirs = jnp.where(here > 0, jnp.exp2((top - peak) * SCALE), 0.0)
            summed = own_n[g, at, :]
            total = summed[:, HD:] * mine + n[:, HD:] * theirs
            out[at, cols] = ((summed[:, :HD] * mine + n[:, :HD] * theirs) / total).astype(BF16)
        return carry

    lax.fori_loop(0, GROUP, anchor_head, 0, unroll=4)
    store_out = pltpu.make_async_copy(out, co_h.at[0], loc.at[4])
    store_out.start()

    total = po[head]
    for dy, dc in KVS:
        source = (y + dy) % NY * NC + (co + dc) % NC
        rcopy(po.at[0], po_recv.at[source], po_ss.at[0], po_rs.at[source], (here, source)).wait_recv()
        total = total + po_recv[source]
    no_ref[...] = total.astype(BF16)

    for group in (q_copies, kv_copies, az, ax):
        for c in group.values():
            c.wait_send()
    for c in n_copies:
        c.wait_send()
    for e in range(NX):
        for c in range(NC):

            @pl.when((x - e + NX) % NX * NC + c != head)
            def _():
                po_copies[e, c].wait_send()

    for d in ZS:

        @pl.when((z + d) % NZ != 0)
        def _():
            spreads[d].wait_send()

    for c in stripes:
        c.wait_send()

    @pl.when(here == NZ)
    def _():
        far_stripe.wait_send()

    @pl.when(z == 0)
    def _():
        for c in scatters:
            c.wait_send()

    store_out.wait()


def body(ctx_query, ctx_kv, new_query, new_kv, out_weight):
    any_space = pl.BlockSpec(memory_space=pltpu.HBM)
    vmem = pl.BlockSpec(memory_space=pltpu.VMEM)
    cols = out_weight.shape[1]
    mine = NCTX * QT // NKV
    dma = pltpu.SemaphoreType.DMA
    return pl.pallas_call(
        kernel,
        out_shape=(
            jax.ShapeDtypeStruct(ctx_query.shape, BF16),
            jax.ShapeDtypeStruct((mine, cols), BF16),
        ),
        in_specs=[any_space, any_space, vmem, vmem, any_space],
        out_specs=(any_space, vmem),
        scratch_shapes=[
            pltpu.VMEM((BLK, GROUP * HD), BF16),
            pltpu.VMEM((NX, 2, BLK, HD), BF16),
            pltpu.VMEM((GROUP * HD, cols), BF16),
            pltpu.VMEM((NX, 2, 16, HD), BF16),
            pltpu.VMEM((NZ, ROWS, HD), BF16),
            pltpu.VMEM((2, BLK, HD), BF16),
            pltpu.VMEM((GROUP, BLK, 2 * HD), F32),
            pltpu.VMEM((GROUP, BLK, HD), F32),
            pltpu.VMEM((BLK, GROUP * HD), BF16),
            pltpu.VMEM((NZ * ROWS, 2 * HD), F32),
            pltpu.VMEM((NZ * ROWS, HD), F32),
            pltpu.VMEM((NZ, ROWS, HD), BF16),
            pltpu.VMEM((NZ, ROWS, HD), BF16),
            pltpu.VMEM((NZ, QT, HD), F32),
            pltpu.VMEM((NZ, QT, HD), F32),
            pltpu.VMEM((NCTX, ROWS, HD), BF16),
            pltpu.VMEM((NKV, mine, cols), F32),
            pltpu.VMEM((NKV, mine, cols), F32),
            dma((5,)),
            dma((NZ,)), dma((NZ,)),
            dma((11,)), dma((11,)),
            dma((2, NZ)), dma((2, NZ)),
            dma((NZ,)), dma((NZ,)),
            dma((NZ,)), dma,
            dma, dma,
            dma((5,)), dma((5,)),
            dma((NZ,)), dma((NZ,)),
            dma((NZ, NX)), dma((NZ, NX)),
            dma((NKV,)), dma((NKV,)),
        ],
        compiler_params=pltpu.CompilerParams(
            collective_id=0, has_side_effects=True, vmem_limit_bytes=60 * 1024 * 1024
        ),
        name="star",
    )(ctx_query, ctx_kv, new_query, new_kv, out_weight)


def solution(mesh):
    return jax.shard_map(
        body,
        mesh=mesh,
        in_specs=(
            P("kv", "ctx", None),
            P(None, "kv", "ctx", None),
            P("kv", "ctx", None),
            P(None, "kv", "ctx", None),
            P("kv", "ctx"),
        ),
        out_specs=(P("kv", "ctx", None), P("kv", "ctx")),
        check_vma=False,
    )
```

```python
import math

import jax
import jax.numpy as jnp
from jax import lax
from jax.experimental import pallas as pl
from jax.experimental.pallas import tpu as pltpu
from jax.sharding import PartitionSpec as P

HD = 128
GROUP = 8
BLK = 512
NX, NZ, NY, NC = 4, 8, 4, 2
NCTX, NKV = NX * NZ, NY * NC
QT = 8
ROWS = QT * GROUP
STRIPE = BLK // NX
PIECE = STRIPE // NZ
SCALE = HD**-0.5 * math.log2(math.e)
LOW = -1e30
ZS = (1, 7, 2, 6, 3, 5, 4)
FAR = ZS[::-1]
SIDES = (1, 3, 2)
KVS = ((0, 1), (1, 0), (3, 0), (1, 1), (3, 1), (2, 0), (2, 1))
F32, BF16 = jnp.float32, jnp.bfloat16


def rcopy(src, dst, send, recv, dev):
    return pltpu.make_async_remote_copy(
        src_ref=src,
        dst_ref=dst,
        send_sem=send,
        recv_sem=recv,
        device_id=dev,
        device_id_type=pl.DeviceIdType.MESH,
    )


def scores(q, k):
    return lax.dot_general(q, k, (((1,), (1,)), ((), ())), preferred_element_type=F32)


def with_ones(v):
    return jnp.concatenate([v, jnp.ones_like(v)], axis=1)


def weigh(s, top, v1):
    return jnp.dot(jnp.exp2((s - top) * SCALE).astype(BF16), v1, preferred_element_type=F32)


def peak_of(s):
    return jnp.max(s, axis=1, keepdims=True)


def kernel(
    cq_h, ckv_h, nq_h, nkv_h, w_h,
    co_h, no_ref,
    cq, kv, w, nq_v, nkv_v, fresh, qbuf, anc, own_n, own_m, out, q_n, q_m,
    n_send, n_recv, st_send, st_recv, att, po, po_recv,
    loc, q_ss, q_rs, kv_ss, kv_rs, n_ss, n_rs, an_ss, an_rs, sc_ss, sc_rs, pass_ss, pass_rs, st_ss, st_rs,
    az_ss, az_rs, ax_ss, ax_rs, po_ss, po_rs,
):
    here = lax.axis_index("ctx")
    head = lax.axis_index("kv")
    x, z, y, co = here // NZ, here % NZ, head // NC, head % NC

    def member(d):
        return (x + 2 * (d % 2)) % NX * NZ + (z + d) % NZ

    colour = (x + 2 * (z % 2)) % NX

    def zdev(d):
        return (member(d), head)

    def side(e):
        if e % 2:
            return ((x + e) % NX * NZ + z, head)
        return (x * NZ + (z + (1 if e == 2 else NZ - 1)) % NZ, head)

    def kvdev(dy, dc):
        return (here, (y + dy) % NY * NC + (co + dc) % NC)

    load_nq = pltpu.make_async_copy(nq_h, nq_v, loc.at[5])
    load_nkv = pltpu.make_async_copy(nkv_h, nkv_v, loc.at[6])
    load_nq.start()
    load_nkv.start()
    barrier = pltpu.get_barrier_semaphore()
    peers = [zdev(d) for d in ZS] + [side(e) for e in (1, 3, 2, 4)] + [kvdev(*k) for k in KVS]
    for dev in peers:
        pl.semaphore_signal(barrier, inc=1, device_id=dev, device_id_type=pl.DeviceIdType.MESH)
    load_kv = pltpu.make_async_copy(ckv_h.at[:, 0], kv.at[0], loc.at[0])
    load_cq = pltpu.make_async_copy(cq_h.at[0], cq, loc.at[1])
    load_w = pltpu.make_async_copy(w_h, w, loc.at[2])
    load_kv.start()
    load_cq.start()
    load_w.start()
    load_nq.wait()
    load_nkv.wait()
    nq = nq_v[0].astype(F32)
    qbuf[0] = jnp.concatenate([nq[:, g * HD : (g + 1) * HD] for g in range(GROUP)], 0).astype(BF16)
    nkv = nkv_v[:, 0].astype(F32)
    fresh[0] = jnp.concatenate([nkv, jnp.zeros_like(nkv)], 1).astype(BF16)
    pl.semaphore_wait(barrier, len(peers))

    q_copies = {d: rcopy(qbuf.at[0], qbuf.at[d], q_ss.at[d], q_rs.at[d], zdev(d)) for d in ZS}
    for d in FAR:
        q_copies[d].start()
    kv_copies = {}

    def send_kv(name, src, dst, dev):
        kv_copies[name] = rcopy(src, dst, kv_ss.at[len(kv_copies)], kv_rs.at[len(kv_copies)], dev)
        kv_copies[name].start()

    for e in SIDES:
        send_kv(("fresh", e), fresh.at[0], fresh.at[e], side(e))
    for part in range(2):
        for e in (1, 3):
            send_kv((part, e), ckv_h.at[part, 0], kv.at[e, part], side(e))
        for e in (2, 4):
            half = pl.ds((e // 2 - 1) * (BLK // 2), BLK // 2)
            send_kv((part, e), ckv_h.at[part, 0, half], kv.at[2, part, half], side(e))

    load_kv.wait()
    load_cq.wait()

    keep = lax.broadcasted_iota(jnp.int32, (128, 128), 1) <= lax.broadcasted_iota(
        jnp.int32, (128, 128), 0
    )

    def own_head(g, carry):
        cols = pl.ds(pl.multiple_of(g * HD, HD), HD)
        tiles = [pl.ds(r * 128, 128) for r in range(4)]
        found = [
            scores(cq[at, cols], kv[0, 0, pl.ds(0, (r + 1) * 128), :]) for r, at in enumerate(tiles)
        ]
        weights = []
        for r, at in enumerate(tiles):
            s = jnp.where(keep, found[r][:, r * 128 :], LOW)
            if r:
                s = jnp.concatenate([found[r][:, : r * 128], s], 1)
            top = peak_of(s)
            weights.append(jnp.exp2((s - top) * SCALE).astype(BF16))
            own_m[g, at, :] = jnp.broadcast_to(top, (128, HD))
        for r, at in enumerate(tiles):
            v1 = with_ones(kv[0, 1, pl.ds(0, (r + 1) * 128), :])
            own_n[g, at, :] = jnp.dot(weights[r], v1, preferred_element_type=F32)
        return carry

    lax.fori_loop(0, GROUP, own_head, 0, unroll=4)

    for d in ZS:
        q_copies[d].wait_recv()
    for e in SIDES:
        kv_copies["fresh", e].wait_recv()
    for part in range(2):
        for e in (2, 4):
            kv_copies[part, e].wait_recv()

    row = lax.broadcasted_iota(jnp.int32, (128, NX * 16), 0)
    col = lax.broadcasted_iota(jnp.int32, (128, NX * 16), 1)
    slot = col // 16
    key_x = jnp.where(slot == 2, x, (x - slot + NX) % NX)
    key_z = jnp.where(slot == 2, (z + NZ - 1) % NZ, z)
    key = (key_x * NZ + key_z) * QT + col % 16
    chunks = range(NZ * ROWS // 128)
    rows = [pl.ds(c * 128, 128) for c in chunks]
    qs = [qbuf[pl.ds(c * 2, 2)].reshape(128, HD) for c in chunks]
    fresh_k = fresh[:, 0].reshape(NX * 16, HD)
    fresh_v = with_ones(fresh[:, 1].reshape(NX * 16, HD))
    found = [(scores(q, fresh_k), scores(q, kv[0, 0]), scores(q, kv[2, 0])) for q in qs]
    for c in chunks:
        came = c * 2 + row // ROWS
        token = ((x + 2 * (came % 2)) % NX * NZ + (z - came + NZ) % NZ) * QT + row % QT
        s = jnp.where((col % 16 < QT) & (key <= token), found[c][0], LOW)
        top = jnp.maximum(jnp.maximum(peak_of(s), peak_of(found[c][1])), peak_of(found[c][2]))
        q_n[rows[c], :] = (
            weigh(s, top, fresh_v)
            + weigh(found[c][1], top, with_ones(kv[0, 1]))
            + weigh(found[c][2], top, with_ones(kv[2, 1]))
        )
        q_m[rows[c], :] = jnp.broadcast_to(top, (128, HD))

    for part in range(2):
        for e in (1, 3):
            kv_copies[part, e].wait_recv()

    def stripe(ref, k):
        return ref.at[:, pl.ds(pl.multiple_of(k * STRIPE, STRIPE), STRIPE)]

    def piece(p):
        return anc.at[:, pl.ds(pl.multiple_of(colour * STRIPE + p * PIECE, PIECE), PIECE)]

    local_stripe = pltpu.make_async_copy(stripe(kv.at[x], x), stripe(anc, x), loc.at[3])
    far_stripe = rcopy(stripe(kv.at[1], 2), stripe(anc, 2), pass_ss, pass_rs, side(1))

    @pl.when((z == 0) & (x != 2))
    def _():
        local_stripe.start()

    @pl.when(here == NZ)
    def _():
        far_stripe.start()

    lane = lax.broadcasted_iota(jnp.int32, (2, QT, HD), 2)
    n_copies = []
    for pair in ((1, 2), (3, 0)):
        found = {c: (scores(qs[c], kv[1, 0]), scores(qs[c], kv[3, 0])) for c in pair}
        for c in pair:
            old = q_m[rows[c], :][:, :1]
            top = jnp.maximum(jnp.maximum(old, peak_of(found[c][0])), peak_of(found[c][1]))
            n = (
                q_n[rows[c], :] * jnp.exp2((old - top) * SCALE)
                + weigh(found[c][0], top, with_ones(kv[1, 1]))
                + weigh(found[c][1], top, with_ones(kv[3, 1]))
            )
            two = pl.ds(2 * c, 2)
            n_send[two] = (n[:, :HD] / n[:, HD:]).astype(BF16).reshape(2, ROWS, HD)
            lse = (top * SCALE + jnp.log2(n[:, HD:])).reshape(2, GROUP, QT, HD)
            stat = lse[:, 0]
            for g in range(1, GROUP):
                stat = jnp.where(lane == g, lse[:, g], stat)
            st_send[two] = stat
        for d in sorted(2 * c + i for c in pair for i in range(2)):
            if d:
                args = (n_ss.at[0, d], n_rs.at[0, d], zdev(NZ - d))
                n_copies.append(rcopy(st_send.at[d], st_recv.at[d], *args))
                args = (n_ss.at[1, d], n_rs.at[1, d], zdev(NZ - d))
                n_copies.append(rcopy(n_send.at[d], n_recv.at[d], *args))
                n_copies[-2].start()
                n_copies[-1].start()

    scatters = [rcopy(piece(p), piece(p), sc_ss.at[p], sc_rs, zdev(p)) for p in range(1, NZ)]

    @pl.when((z == 0) & (x != 2))
    def _():
        local_stripe.wait()

    @pl.when(here == 2 * NZ)
    def _():
        far_stripe.wait_recv()

    @pl.when(z == 0)
    def _():
        for c in scatters:
            c.start()

    for c in n_copies:
        c.wait_recv()
    st_recv[0] = st_send[0]
    n_recv[0] = n_send[0]
    stats = st_recv[...]
    peak = jnp.max(stats, axis=0)
    share = jnp.exp2(stats - peak[None])
    share = share / jnp.sum(share, axis=0)[None]
    parts = n_recv[...].astype(F32)
    pieces = []
    for g in range(GROUP):
        pieces.append(jnp.sum(parts[:, g * QT : (g + 1) * QT] * share[:, :, g : g + 1], axis=0))
    att[here] = jnp.concatenate(pieces, 0).astype(BF16)

    az = {d: rcopy(att.at[here], att.at[here], az_ss.at[d], az_rs.at[d], zdev(d)) for d in ZS}
    for d in FAR:
        az[d].start()
    ax = {}

    def forward(d):
        block = member(NZ - d)
        for e in SIDES:
            dev = side(4) if e == 2 and d % 2 else side(e)
            ax[d, e] = rcopy(att.at[block], att.at[block], ax_ss.at[d, e], ax_rs.at[d, e], dev)
            ax[d, e].start()

    forward(0)

    @pl.when(z > 0)
    def _():
        rcopy(piece(0), piece(z), sc_ss.at[0], sc_rs, zdev(1)).wait_recv()

    spreads = {d: rcopy(piece(z), piece(z), an_ss.at[d], an_rs.at[d], zdev(d)) for d in ZS}
    for d in FAR:

        @pl.when((z + d) % NZ != 0)
        def _():
            spreads[d].start()

    for d in ZS:
        az[d].wait_recv()
        forward(d)

    @pl.when(z > 0)
    def _():
        for d in ZS:
            spreads[d].wait_recv()

    stripes = []
    for e in (1, 3):
        mine = stripe(anc, colour)
        stripes.append(rcopy(mine, mine, st_ss.at[e], st_rs.at[e], side(e)))
    for e in (2, 4):
        first = colour * STRIPE + (e // 2 - 1) * (STRIPE // 2)
        mine = anc.at[:, pl.ds(pl.multiple_of(first, STRIPE // 2), STRIPE // 2)]
        stripes.append(rcopy(mine, mine, st_ss.at[e], st_rs.at[e], side(e)))
    for c in stripes:
        c.start()

    load_w.wait()
    mine = NCTX * QT // NKV
    po_copies = {}

    def project(e):
        block = (x - e + NX) % NX
        lhs = att[pl.ds(block * NZ, NZ)].astype(F32)
        acc = jnp.zeros((NZ * QT, no_ref.shape[1]), F32)
        for j in range(GROUP // 2):
            pair = [lhs[:, g * QT : (g + 1) * QT].reshape(NZ * QT, HD) for g in (2 * j, 2 * j + 1)]
            acc = acc + jnp.dot(
                jnp.concatenate(pair, 1).astype(BF16),
                w[pl.ds(j * 2 * HD, 2 * HD), :],
                preferred_element_type=F32,
            )
        po[pl.ds(block * NC, NC)] = acc.reshape(NC, mine, acc.shape[1])
        for c in range(NC):
            dest = block * NC + c
            po_copies[e, c] = rcopy(
                po.at[dest], po_recv.at[head], po_ss.at[e * NC + c], po_rs.at[head], (here, dest)
            )

            @pl.when(dest != head)
            def _():
                po_copies[e, c].start()

    for d in (0,) + ZS:
        ax[d, 2].wait_recv()
    project(0)
    project(2)
    for d in (0,) + ZS:
        ax[d, 1].wait_recv()
        ax[d, 3].wait_recv()
    project(1)
    project(3)

    for c in stripes:
        c.wait_recv()

    def anchor_head(g, carry):
        cols = pl.ds(pl.multiple_of(g * HD, HD), HD)
        for r in range(4):
            at = pl.ds(r * 128, 128)
            s = scores(cq[at, cols], anc[0])
            top = peak_of(s)
            n = weigh(s, top, with_ones(anc[1]))
            old = own_m[g, at, :]
            peak = jnp.maximum(old, top)
            mine = jnp.where(here > 0, jnp.exp2((old - peak) * SCALE), 1.0)
            theirs = jnp.where(here > 0, jnp.exp2((top - peak) * SCALE), 0.0)
            summed = own_n[g, at, :]
            total = summed[:, HD:] * mine + n[:, HD:] * theirs
            out[at, cols] = ((summed[:, :HD] * mine + n[:, :HD] * theirs) / total).astype(BF16)
        return carry

    lax.fori_loop(0, GROUP, anchor_head, 0, unroll=4)
    store_out = pltpu.make_async_copy(out, co_h.at[0], loc.at[4])
    store_out.start()

    total = po[head]
    for dy, dc in KVS:
        source = (y + dy) % NY * NC + (co + dc) % NC
        rcopy(po.at[0], po_recv.at[source], po_ss.at[0], po_rs.at[source], (here, source)).wait_recv()
        total = total + po_recv[source]
    no_ref[...] = total.astype(BF16)

    for group in (q_copies, kv_copies, az, ax):
        for c in group.values():
            c.wait_send()
    for c in n_copies:
        c.wait_send()
    for e in range(NX):
        for c in range(NC):

            @pl.when((x - e + NX) % NX * NC + c != head)
            def _():
                po_copies[e, c].wait_send()

    for d in ZS:

        @pl.when((z + d) % NZ != 0)
        def _():
            spreads[d].wait_send()

    for c in stripes:
        c.wait_send()

    @pl.when(here == NZ)
    def _():
        far_stripe.wait_send()

    @pl.when(z == 0)
    def _():
        for c in scatters:
            c.wait_send()

    store_out.wait()


def body(ctx_query, ctx_kv, new_query, new_kv, out_weight):
    any_space = pl.BlockSpec(memory_space=pltpu.HBM)
    vmem = pl.BlockSpec(memory_space=pltpu.VMEM)
    cols = out_weight.shape[1]
    mine = NCTX * QT // NKV
    dma = pltpu.SemaphoreType.DMA
    return pl.pallas_call(
        kernel,
        out_shape=(
            jax.ShapeDtypeStruct(ctx_query.shape, BF16),
            jax.ShapeDtypeStruct((mine, cols), BF16),
        ),
        in_specs=[any_space] * 5,
        out_specs=(any_space, vmem),
        scratch_shapes=[
            pltpu.VMEM((BLK, GROUP * HD), BF16),
            pltpu.VMEM((NX, 2, BLK, HD), BF16),
            pltpu.VMEM((GROUP * HD, cols), BF16),
            pltpu.VMEM(new_query.shape, BF16),
            pltpu.VMEM(new_kv.shape, BF16),
            pltpu.VMEM((NX, 2, 16, HD), BF16),
            pltpu.VMEM((NZ, ROWS, HD), BF16),
            pltpu.VMEM((2, BLK, HD), BF16),
            pltpu.VMEM((GROUP, BLK, 2 * HD), F32),
            pltpu.VMEM((GROUP, BLK, HD), F32),
            pltpu.VMEM((BLK, GROUP * HD), BF16),
            pltpu.VMEM((NZ * ROWS, 2 * HD), F32),
            pltpu.VMEM((NZ * ROWS, HD), F32),
            pltpu.VMEM((NZ, ROWS, HD), BF16),
            pltpu.VMEM((NZ, ROWS, HD), BF16),
            pltpu.VMEM((NZ, QT, HD), F32),
            pltpu.VMEM((NZ, QT, HD), F32),
            pltpu.VMEM((NCTX, ROWS, HD), BF16),
            pltpu.VMEM((NKV, mine, cols), F32),
            pltpu.VMEM((NKV, mine, cols), F32),
            dma((7,)),
            dma((NZ,)), dma((NZ,)),
            dma((11,)), dma((11,)),
            dma((2, NZ)), dma((2, NZ)),
            dma((NZ,)), dma((NZ,)),
            dma((NZ,)), dma,
            dma, dma,
            dma((5,)), dma((5,)),
            dma((NZ,)), dma((NZ,)),
            dma((NZ, NX)), dma((NZ, NX)),
            dma((NKV,)), dma((NKV,)),
        ],
        compiler_params=pltpu.CompilerParams(
            collective_id=0, has_side_effects=True, vmem_limit_bytes=60 * 1024 * 1024
        ),
        name="star",
    )(ctx_query, ctx_kv, new_query, new_kv, out_weight)


def solution(mesh):
    return jax.shard_map(
        body,
        mesh=mesh,
        in_specs=(
            P("kv", "ctx", None),
            P(None, "kv", "ctx", None),
            P("kv", "ctx", None),
            P(None, "kv", "ctx", None),
            P("kv", "ctx"),
        ),
        out_specs=(P("kv", "ctx", None), P("kv", "ctx")),
        check_vma=False,
    )
```

```python
import math

import jax
import jax.numpy as jnp
from jax import lax
from jax.experimental import pallas as pl
from jax.experimental.pallas import tpu as pltpu
from jax.sharding import PartitionSpec as P

HD = 128
GROUP = 8
BLK = 512
NX, NZ, NY, NC = 4, 8, 4, 2
NCTX, NKV = NX * NZ, NY * NC
QT = 8
ROWS = QT * GROUP
STRIPE = BLK // NX
PIECE = STRIPE // NZ
SCALE = HD**-0.5 * math.log2(math.e)
LOW = -1e30
ZS = (1, 7, 2, 6, 3, 5, 4)
FAR = ZS[::-1]
SIDES = (1, 3, 2)
KVS = ((0, 1), (1, 0), (3, 0), (1, 1), (3, 1), (2, 0), (2, 1))
F32, BF16 = jnp.float32, jnp.bfloat16


def rcopy(src, dst, send, recv, dev):
    return pltpu.make_async_remote_copy(
        src_ref=src,
        dst_ref=dst,
        send_sem=send,
        recv_sem=recv,
        device_id=dev,
        device_id_type=pl.DeviceIdType.MESH,
    )


def scores(q, k):
    return lax.dot_general(q, k, (((1,), (1,)), ((), ())), preferred_element_type=F32)


def with_ones(v):
    return jnp.concatenate([v, jnp.ones_like(v)], axis=1)


def weigh(s, top, v1):
    return jnp.dot(jnp.exp2((s - top) * SCALE).astype(BF16), v1, preferred_element_type=F32)


def peak_of(s):
    return jnp.max(s, axis=1, keepdims=True)


def kernel(
    cq_h, ckv_h, nq_h, nkv_h, w_h,
    co_h, no_h,
    cq, kv, w, nq_v, nkv_v, fresh, qbuf, anc, own_n, own_m, out, q_n, q_m,
    n_send, n_recv, st_send, st_recv, att, po, po_recv, no_v,
    loc, q_ss, q_rs, kv_ss, kv_rs, n_ss, n_rs, an_ss, an_rs, sc_ss, sc_rs, pass_ss, pass_rs, st_ss, st_rs,
    az_ss, az_rs, ax_ss, ax_rs, po_ss, po_rs,
):
    here = lax.axis_index("ctx")
    head = lax.axis_index("kv")
    x, z, y, co = here // NZ, here % NZ, head // NC, head % NC

    def member(d):
        return (x + 2 * (d % 2)) % NX * NZ + (z + d) % NZ

    colour = (x + 2 * (z % 2)) % NX

    def zdev(d):
        return (member(d), head)

    def side(e):
        if e % 2:
            return ((x + e) % NX * NZ + z, head)
        return (x * NZ + (z + (1 if e == 2 else NZ - 1)) % NZ, head)

    def kvdev(dy, dc):
        return (here, (y + dy) % NY * NC + (co + dc) % NC)

    load_nq = pltpu.make_async_copy(nq_h, nq_v, loc.at[5])
    load_nkv = pltpu.make_async_copy(nkv_h, nkv_v, loc.at[6])
    load_nq.start()
    load_nkv.start()
    barrier = pltpu.get_barrier_semaphore()
    peers = [zdev(d) for d in ZS] + [side(e) for e in (1, 3, 2, 4)] + [kvdev(*k) for k in KVS]
    for dev in peers:
        pl.semaphore_signal(barrier, inc=1, device_id=dev, device_id_type=pl.DeviceIdType.MESH)
    load_kv = pltpu.make_async_copy(ckv_h.at[:, 0], kv.at[0], loc.at[0])
    load_cq = pltpu.make_async_copy(cq_h.at[0], cq, loc.at[1])
    load_w = pltpu.make_async_copy(w_h, w, loc.at[2])
    load_kv.start()
    load_cq.start()
    load_w.start()
    load_nq.wait()
    load_nkv.wait()
    nq = nq_v[0].astype(F32)
    qbuf[0] = jnp.concatenate([nq[:, g * HD : (g + 1) * HD] for g in range(GROUP)], 0).astype(BF16)
    nkv = nkv_v[:, 0].astype(F32)
    fresh[0] = jnp.concatenate([nkv, jnp.zeros_like(nkv)], 1).astype(BF16)
    pl.semaphore_wait(barrier, len(peers))

    q_copies = {d: rcopy(qbuf.at[0], qbuf.at[d], q_ss.at[d], q_rs.at[d], zdev(d)) for d in ZS}
    for d in FAR:
        q_copies[d].start()
    kv_copies = {}

    def send_kv(name, src, dst, dev):
        kv_copies[name] = rcopy(src, dst, kv_ss.at[len(kv_copies)], kv_rs.at[len(kv_copies)], dev)
        kv_copies[name].start()

    for e in SIDES:
        send_kv(("fresh", e), fresh.at[0], fresh.at[e], side(e))
    for part in range(2):
        for e in (1, 3):
            send_kv((part, e), ckv_h.at[part, 0], kv.at[e, part], side(e))
        for e in (2, 4):
            half = pl.ds((e // 2 - 1) * (BLK // 2), BLK // 2)
            send_kv((part, e), ckv_h.at[part, 0, half], kv.at[2, part, half], side(e))

    load_kv.wait()
    load_cq.wait()

    keep = lax.broadcasted_iota(jnp.int32, (128, 128), 1) <= lax.broadcasted_iota(
        jnp.int32, (128, 128), 0
    )

    def own_head(g, carry):
        cols = pl.ds(pl.multiple_of(g * HD, HD), HD)
        tiles = [pl.ds(r * 128, 128) for r in range(4)]
        found = [
            scores(cq[at, cols], kv[0, 0, pl.ds(0, (r + 1) * 128), :]) for r, at in enumerate(tiles)
        ]
        weights = []
        for r, at in enumerate(tiles):
            s = jnp.where(keep, found[r][:, r * 128 :], LOW)
            if r:
                s = jnp.concatenate([found[r][:, : r * 128], s], 1)
            top = peak_of(s)
            weights.append(jnp.exp2((s - top) * SCALE).astype(BF16))
            own_m[g, at, :] = jnp.broadcast_to(top, (128, HD))
        for r, at in enumerate(tiles):
            v1 = with_ones(kv[0, 1, pl.ds(0, (r + 1) * 128), :])
            own_n[g, at, :] = jnp.dot(weights[r], v1, preferred_element_type=F32)
        return carry

    lax.fori_loop(0, GROUP, own_head, 0, unroll=4)

    for d in ZS:
        q_copies[d].wait_recv()
    for e in SIDES:
        kv_copies["fresh", e].wait_recv()
    for part in range(2):
        for e in (2, 4):
            kv_copies[part, e].wait_recv()

    row = lax.broadcasted_iota(jnp.int32, (128, NX * 16), 0)
    col = lax.broadcasted_iota(jnp.int32, (128, NX * 16), 1)
    slot = col // 16
    key_x = jnp.where(slot == 2, x, (x - slot + NX) % NX)
    key_z = jnp.where(slot == 2, (z + NZ - 1) % NZ, z)
    key = (key_x * NZ + key_z) * QT + col % 16
    chunks = range(NZ * ROWS // 128)
    rows = [pl.ds(c * 128, 128) for c in chunks]
    qs = [qbuf[pl.ds(c * 2, 2)].reshape(128, HD) for c in chunks]
    fresh_k = fresh[:, 0].reshape(NX * 16, HD)
    fresh_v = with_ones(fresh[:, 1].reshape(NX * 16, HD))
    found = [(scores(q, fresh_k), scores(q, kv[0, 0]), scores(q, kv[2, 0])) for q in qs]
    for c in chunks:
        came = c * 2 + row // ROWS
        token = ((x + 2 * (came % 2)) % NX * NZ + (z - came + NZ) % NZ) * QT + row % QT
        s = jnp.where((col % 16 < QT) & (key <= token), found[c][0], LOW)
        top = jnp.maximum(jnp.maximum(peak_of(s), peak_of(found[c][1])), peak_of(found[c][2]))
        q_n[rows[c], :] = (
            weigh(s, top, fresh_v)
            + weigh(found[c][1], top, with_ones(kv[0, 1]))
            + weigh(found[c][2], top, with_ones(kv[2, 1]))
        )
        q_m[rows[c], :] = jnp.broadcast_to(top, (128, HD))

    for part in range(2):
        for e in (1, 3):
            kv_copies[part, e].wait_recv()

    def stripe(ref, k):
        return ref.at[:, pl.ds(pl.multiple_of(k * STRIPE, STRIPE), STRIPE)]

    def piece(p):
        return anc.at[:, pl.ds(pl.multiple_of(colour * STRIPE + p * PIECE, PIECE), PIECE)]

    local_stripe = pltpu.make_async_copy(stripe(kv.at[x], x), stripe(anc, x), loc.at[3])
    far_stripe = rcopy(stripe(kv.at[1], 2), stripe(anc, 2), pass_ss, pass_rs, side(1))

    @pl.when((z == 0) & (x != 2))
    def _():
        local_stripe.start()

    @pl.when(here == NZ)
    def _():
        far_stripe.start()

    lane = lax.broadcasted_iota(jnp.int32, (2, QT, HD), 2)
    n_copies = []
    for pair in ((1, 2), (3, 0)):
        found = {c: (scores(qs[c], kv[1, 0]), scores(qs[c], kv[3, 0])) for c in pair}
        for c in pair:
            old = q_m[rows[c], :][:, :1]
            top = jnp.maximum(jnp.maximum(old, peak_of(found[c][0])), peak_of(found[c][1]))
            n = (
                q_n[rows[c], :] * jnp.exp2((old - top) * SCALE)
                + weigh(found[c][0], top, with_ones(kv[1, 1]))
                + weigh(found[c][1], top, with_ones(kv[3, 1]))
            )
            two = pl.ds(2 * c, 2)
            n_send[two] = (n[:, :HD] / n[:, HD:]).astype(BF16).reshape(2, ROWS, HD)
            lse = (top * SCALE + jnp.log2(n[:, HD:])).reshape(2, GROUP, QT, HD)
            stat = lse[:, 0]
            for g in range(1, GROUP):
                stat = jnp.where(lane == g, lse[:, g], stat)
            st_send[two] = stat
        for d in sorted(2 * c + i for c in pair for i in range(2)):
            if d:
                args = (n_ss.at[0, d], n_rs.at[0, d], zdev(NZ - d))
                n_copies.append(rcopy(st_send.at[d], st_recv.at[d], *args))
                args = (n_ss.at[1, d], n_rs.at[1, d], zdev(NZ - d))
                n_copies.append(rcopy(n_send.at[d], n_recv.at[d], *args))
                n_copies[-2].start()
                n_copies[-1].start()

    scatters = [rcopy(piece(p), piece(p), sc_ss.at[p], sc_rs, zdev(p)) for p in range(1, NZ)]

    @pl.when((z == 0) & (x != 2))
    def _():
        local_stripe.wait()

    @pl.when(here == 2 * NZ)
    def _():
        far_stripe.wait_recv()

    @pl.when(z == 0)
    def _():
        for c in scatters:
            c.start()

    for c in n_copies:
        c.wait_recv()
    st_recv[0] = st_send[0]
    n_recv[0] = n_send[0]
    stats = st_recv[...]
    peak = jnp.max(stats, axis=0)
    share = jnp.exp2(stats - peak[None])
    share = share / jnp.sum(share, axis=0)[None]
    parts = n_recv[...].astype(F32)
    pieces = []
    for g in range(GROUP):
        pieces.append(jnp.sum(parts[:, g * QT : (g + 1) * QT] * share[:, :, g : g + 1], axis=0))
    att[here] = jnp.concatenate(pieces, 0).astype(BF16)

    az = {d: rcopy(att.at[here], att.at[here], az_ss.at[d], az_rs.at[d], zdev(d)) for d in ZS}
    for d in FAR:
        az[d].start()
    ax = {}

    def forward(d):
        block = member(NZ - d)
        for e in SIDES:
            dev = side(4) if e == 2 and d % 2 else side(e)
            ax[d, e] = rcopy(att.at[block], att.at[block], ax_ss.at[d, e], ax_rs.at[d, e], dev)
            ax[d, e].start()

    forward(0)

    @pl.when(z > 0)
    def _():
        rcopy(piece(0), piece(z), sc_ss.at[0], sc_rs, zdev(1)).wait_recv()

    spreads = {d: rcopy(piece(z), piece(z), an_ss.at[d], an_rs.at[d], zdev(d)) for d in ZS}
    for d in FAR:

        @pl.when((z + d) % NZ != 0)
        def _():
            spreads[d].start()

    for d in ZS:
        az[d].wait_recv()
        forward(d)

    @pl.when(z > 0)
    def _():
        for d in ZS:
            spreads[d].wait_recv()

    stripes = []
    for e in (1, 3):
        mine = stripe(anc, colour)
        stripes.append(rcopy(mine, mine, st_ss.at[e], st_rs.at[e], side(e)))
    for e in (2, 4):
        first = colour * STRIPE + (e // 2 - 1) * (STRIPE // 2)
        mine = anc.at[:, pl.ds(pl.multiple_of(first, STRIPE // 2), STRIPE // 2)]
        stripes.append(rcopy(mine, mine, st_ss.at[e], st_rs.at[e], side(e)))
    for c in stripes:
        c.start()

    load_w.wait()
    mine = NCTX * QT // NKV
    po_copies = {}

    def project(first, second):
        blocks = [(x - e + NX) % NX for e in (first, second)]
        lhs = [att[pl.ds(b * NZ, NZ)].astype(F32) for b in blocks]
        acc = jnp.zeros((2 * NZ * QT, no_v.shape[1]), F32)
        for j in range(GROUP // 2):
            pair = [
                jnp.concatenate([a[:, g * QT : (g + 1) * QT].reshape(NZ * QT, HD) for a in lhs], 0)
                for g in (2 * j, 2 * j + 1)
            ]
            acc = acc + jnp.dot(
                jnp.concatenate(pair, 1).astype(BF16),
                w[pl.ds(j * 2 * HD, 2 * HD), :],
                preferred_element_type=F32,
            )
        for i, e in enumerate((first, second)):
            rows = acc[i * NZ * QT : (i + 1) * NZ * QT]
            po[pl.ds(blocks[i] * NC, NC)] = rows.reshape(NC, mine, acc.shape[1]).astype(BF16)
            for c in range(NC):
                dest = blocks[i] * NC + c
                po_copies[e, c] = rcopy(
                    po.at[dest], po_recv.at[head], po_ss.at[e * NC + c], po_rs.at[head], (here, dest)
                )

                @pl.when(dest != head)
                def _():
                    po_copies[e, c].start()

    for d in (0,) + ZS:
        ax[d, 2].wait_recv()
    project(0, 2)
    for d in (0,) + ZS:
        ax[d, 1].wait_recv()
        ax[d, 3].wait_recv()
    project(1, 3)

    for c in stripes:
        c.wait_recv()

    def anchor_head(g, carry):
        cols = pl.ds(pl.multiple_of(g * HD, HD), HD)
        for r in range(4):
            at = pl.ds(r * 128, 128)
            s = scores(cq[at, cols], anc[0])
            top = peak_of(s)
            n = weigh(s, top, with_ones(anc[1]))
            old = own_m[g, at, :]
            peak = jnp.maximum(old, top)
            mine = jnp.where(here > 0, jnp.exp2((old - peak) * SCALE), 1.0)
            theirs = jnp.where(here > 0, jnp.exp2((top - peak) * SCALE), 0.0)
            summed = own_n[g, at, :]
            total = summed[:, HD:] * mine + n[:, HD:] * theirs
            out[at, cols] = ((summed[:, :HD] * mine + n[:, :HD] * theirs) / total).astype(BF16)
        return carry

    half = GROUP * HD // 2
    stores = []

    def anchor_half(i):
        lax.fori_loop(i * GROUP // 2, (i + 1) * GROUP // 2, anchor_head, 0, unroll=4)
        at = pl.ds(i * half, half)
        stores.append(pltpu.make_async_copy(out.at[:, at], co_h.at[0, :, at], loc.at[4 + 3 * i]))
        stores[i].start()

    anchor_half(0)
    anchor_half(1)
    total = po[head].astype(F32)
    for dy, dc in KVS:
        source = (y + dy) % NY * NC + (co + dc) % NC
        rcopy(po.at[0], po_recv.at[source], po_ss.at[0], po_rs.at[source], (here, source)).wait_recv()
        total = total + po_recv[source].astype(F32)
    no_v[...] = total.astype(BF16)

    store_new = pltpu.make_async_copy(no_v, no_h, loc.at[0])
    store_new.start()
    for group in (q_copies, kv_copies, az, ax):
        for c in group.values():
            c.wait_send()
    for c in n_copies:
        c.wait_send()
    for e in range(NX):
        for c in range(NC):

            @pl.when((x - e + NX) % NX * NC + c != head)
            def _():
                po_copies[e, c].wait_send()

    for d in ZS:

        @pl.when((z + d) % NZ != 0)
        def _():
            spreads[d].wait_send()

    for c in stripes:
        c.wait_send()

    @pl.when(here == NZ)
    def _():
        far_stripe.wait_send()

    @pl.when(z == 0)
    def _():
        for c in scatters:
            c.wait_send()

    for c in stores:
        c.wait()
    store_new.wait()


def body(ctx_query, ctx_kv, new_query, new_kv, out_weight):
    any_space = pl.BlockSpec(memory_space=pltpu.HBM)
    cols = out_weight.shape[1]
    mine = NCTX * QT // NKV
    dma = pltpu.SemaphoreType.DMA
    return pl.pallas_call(
        kernel,
        out_shape=(
            jax.ShapeDtypeStruct(ctx_query.shape, BF16),
            jax.ShapeDtypeStruct((mine, cols), BF16),
        ),
        in_specs=[any_space] * 5,
        out_specs=(any_space, any_space),
        scratch_shapes=[
            pltpu.VMEM((BLK, GROUP * HD), BF16),
            pltpu.VMEM((NX, 2, BLK, HD), BF16),
            pltpu.VMEM((GROUP * HD, cols), BF16),
            pltpu.VMEM(new_query.shape, BF16),
            pltpu.VMEM(new_kv.shape, BF16),
            pltpu.VMEM((NX, 2, 16, HD), BF16),
            pltpu.VMEM((NZ, ROWS, HD), BF16),
            pltpu.VMEM((2, BLK, HD), BF16),
            pltpu.VMEM((GROUP, BLK, 2 * HD), F32),
            pltpu.VMEM((GROUP, BLK, HD), F32),
            pltpu.VMEM((BLK, GROUP * HD), BF16),
            pltpu.VMEM((NZ * ROWS, 2 * HD), F32),
            pltpu.VMEM((NZ * ROWS, HD), F32),
            pltpu.VMEM((NZ, ROWS, HD), BF16),
            pltpu.VMEM((NZ, ROWS, HD), BF16),
            pltpu.VMEM((NZ, QT, HD), F32),
            pltpu.VMEM((NZ, QT, HD), F32),
            pltpu.VMEM((NCTX, ROWS, HD), BF16),
            pltpu.VMEM((NKV, mine, cols), BF16),
            pltpu.VMEM((NKV, mine, cols), BF16),
            pltpu.VMEM((mine, cols), BF16),
            dma((8,)),
            dma((NZ,)), dma((NZ,)),
            dma((11,)), dma((11,)),
            dma((2, NZ)), dma((2, NZ)),
            dma((NZ,)), dma((NZ,)),
            dma((NZ,)), dma,
            dma, dma,
            dma((5,)), dma((5,)),
            dma((NZ,)), dma((NZ,)),
            dma((NZ, NX)), dma((NZ, NX)),
            dma((NKV,)), dma((NKV,)),
        ],
        compiler_params=pltpu.CompilerParams(
            collective_id=0, has_side_effects=True, vmem_limit_bytes=60 * 1024 * 1024
        ),
        name="star",
    )(ctx_query, ctx_kv, new_query, new_kv, out_weight)


def solution(mesh):
    return jax.shard_map(
        body,
        mesh=mesh,
        in_specs=(
            P("kv", "ctx", None),
            P(None, "kv", "ctx", None),
            P("kv", "ctx", None),
            P(None, "kv", "ctx", None),
            P("kv", "ctx"),
        ),
        out_specs=(P("kv", "ctx", None), P("kv", "ctx")),
        check_vma=False,
    )
```

```python
import math

import jax
import jax.numpy as jnp
from jax import lax
from jax.experimental import pallas as pl
from jax.experimental.pallas import tpu as pltpu
from jax.sharding import PartitionSpec as P

HD = 128
GROUP = 8
BLK = 512
NX, NZ, NY, NC = 4, 8, 4, 2
NCTX, NKV = NX * NZ, NY * NC
QT = 8
ROWS = QT * GROUP
STRIPE = BLK // NX
PIECE = STRIPE // NZ
SCALE = HD**-0.5 * math.log2(math.e)
LOW = -1e30
ZS = (1, 7, 2, 6, 3, 5, 4)
FAR = ZS[::-1]
SIDES = (1, 3, 2)
KVS = ((0, 1), (1, 0), (3, 0), (1, 1), (3, 1), (2, 0), (2, 1))
F32, BF16 = jnp.float32, jnp.bfloat16


def rcopy(src, dst, send, recv, dev):
    return pltpu.make_async_remote_copy(
        src_ref=src,
        dst_ref=dst,
        send_sem=send,
        recv_sem=recv,
        device_id=dev,
        device_id_type=pl.DeviceIdType.MESH,
    )


def scores(q, k):
    return lax.dot_general(q, k, (((1,), (1,)), ((), ())), preferred_element_type=F32)


def with_ones(v):
    return jnp.concatenate([v, jnp.ones_like(v)], axis=1)


def weigh(s, top, v1):
    return jnp.dot(jnp.exp2((s - top) * SCALE).astype(BF16), v1, preferred_element_type=F32)


def peak_of(s):
    return jnp.max(s, axis=1, keepdims=True)


def kernel(
    cq_h, ckv_h, nq_h, nkv_h, w_h,
    co_h, no_h,
    cq, kv, w, nq_v, nkv_v, fresh, qbuf, anc, own_n, own_m, out, q_n, q_m,
    n_send, n_recv, st_send, st_recv, att, po, po_recv, no_v,
    loc, q_ss, q_rs, kv_ss, kv_rs, n_ss, n_rs, an_ss, an_rs, sc_ss, sc_rs, pass_ss, pass_rs, st_ss, st_rs,
    az_ss, az_rs, ax_ss, ax_rs, po_ss, po_rs,
):
    here = lax.axis_index("ctx")
    head = lax.axis_index("kv")
    x, z, y, co = here // NZ, here % NZ, head // NC, head % NC

    def member(d):
        return (x + 2 * (d % 2)) % NX * NZ + (z + d) % NZ

    colour = (x + 2 * (z % 2)) % NX

    def zdev(d):
        return (member(d), head)

    def side(e):
        if e % 2:
            return ((x + e) % NX * NZ + z, head)
        return (x * NZ + (z + (1 if e == 2 else NZ - 1)) % NZ, head)

    def kvdev(dy, dc):
        return (here, (y + dy) % NY * NC + (co + dc) % NC)

    load_nq = pltpu.make_async_copy(nq_h, nq_v, loc.at[5])
    load_nkv = pltpu.make_async_copy(nkv_h, nkv_v, loc.at[6])
    load_nq.start()
    load_nkv.start()
    barrier = pltpu.get_barrier_semaphore()
    peers = [zdev(d) for d in ZS] + [side(e) for e in (1, 3, 2, 4)] + [kvdev(*k) for k in KVS]
    for dev in peers:
        pl.semaphore_signal(barrier, inc=1, device_id=dev, device_id_type=pl.DeviceIdType.MESH)
    load_kv = pltpu.make_async_copy(ckv_h.at[:, 0], kv.at[0], loc.at[0])
    load_cq = pltpu.make_async_copy(cq_h.at[0], cq, loc.at[1])
    load_w = pltpu.make_async_copy(w_h, w, loc.at[2])
    load_kv.start()
    load_cq.start()
    load_w.start()
    load_nq.wait()
    load_nkv.wait()
    nq = nq_v[0].astype(F32)
    qbuf[0] = jnp.concatenate([nq[:, g * HD : (g + 1) * HD] for g in range(GROUP)], 0).astype(BF16)
    nkv = nkv_v[:, 0].astype(F32)
    fresh[0] = jnp.concatenate([nkv, jnp.zeros_like(nkv)], 1).astype(BF16)
    pl.semaphore_wait(barrier, len(peers))

    q_copies = {d: rcopy(qbuf.at[0], qbuf.at[d], q_ss.at[d], q_rs.at[d], zdev(d)) for d in ZS}
    for d in FAR:
        q_copies[d].start()
    kv_copies = {}

    def send_kv(name, src, dst, dev):
        kv_copies[name] = rcopy(src, dst, kv_ss.at[len(kv_copies)], kv_rs.at[len(kv_copies)], dev)
        kv_copies[name].start()

    for e in SIDES:
        send_kv(("fresh", e), fresh.at[0], fresh.at[e], side(e))
    for part in range(2):
        for e in (1, 3):
            send_kv((part, e), ckv_h.at[part, 0], kv.at[e, part], side(e))
        for e in (2, 4):
            half = pl.ds((e // 2 - 1) * (BLK // 2), BLK // 2)
            send_kv((part, e), ckv_h.at[part, 0, half], kv.at[2, part, half], side(e))

    load_kv.wait()
    load_cq.wait()

    keep = lax.broadcasted_iota(jnp.int32, (128, 128), 1) <= lax.broadcasted_iota(
        jnp.int32, (128, 128), 0
    )

    def own_head(g, carry):
        cols = pl.ds(pl.multiple_of(g * HD, HD), HD)
        tiles = [pl.ds(r * 128, 128) for r in range(4)]
        found = [
            scores(cq[at, cols], kv[0, 0, pl.ds(0, (r + 1) * 128), :]) for r, at in enumerate(tiles)
        ]
        weights = []
        for r, at in enumerate(tiles):
            s = jnp.where(keep, found[r][:, r * 128 :], LOW)
            if r:
                s = jnp.concatenate([found[r][:, : r * 128], s], 1)
            top = peak_of(s)
            weights.append(jnp.exp2((s - top) * SCALE).astype(BF16))
            own_m[g, at, :] = jnp.broadcast_to(top, (128, HD))
        for r, at in enumerate(tiles):
            v1 = with_ones(kv[0, 1, pl.ds(0, (r + 1) * 128), :])
            own_n[g, at, :] = jnp.dot(weights[r], v1, preferred_element_type=F32)
        return carry

    lax.fori_loop(0, GROUP, own_head, 0, unroll=4)

    for d in ZS:
        q_copies[d].wait_recv()
    for e in SIDES:
        kv_copies["fresh", e].wait_recv()
    for part in range(2):
        for e in (2, 4):
            kv_copies[part, e].wait_recv()

    row = lax.broadcasted_iota(jnp.int32, (128, NX * 16), 0)
    col = lax.broadcasted_iota(jnp.int32, (128, NX * 16), 1)
    slot = col // 16
    key_x = jnp.where(slot == 2, x, (x - slot + NX) % NX)
    key_z = jnp.where(slot == 2, (z + NZ - 1) % NZ, z)
    key = (key_x * NZ + key_z) * QT + col % 16
    chunks = range(NZ * ROWS // 128)
    rows = [pl.ds(c * 128, 128) for c in chunks]
    qs = [qbuf[pl.ds(c * 2, 2)].reshape(128, HD) for c in chunks]
    fresh_k = fresh[:, 0].reshape(NX * 16, HD)
    fresh_v = with_ones(fresh[:, 1].reshape(NX * 16, HD))
    found = [(scores(q, fresh_k), scores(q, kv[0, 0]), scores(q, kv[2, 0])) for q in qs]
    for c in chunks:
        came = c * 2 + row // ROWS
        token = ((x + 2 * (came % 2)) % NX * NZ + (z - came + NZ) % NZ) * QT + row % QT
        s = jnp.where((col % 16 < QT) & (key <= token), found[c][0], LOW)
        top = jnp.maximum(jnp.maximum(peak_of(s), peak_of(found[c][1])), peak_of(found[c][2]))
        q_n[rows[c], :] = (
            weigh(s, top, fresh_v)
            + weigh(found[c][1], top, with_ones(kv[0, 1]))
            + weigh(found[c][2], top, with_ones(kv[2, 1]))
        )
        q_m[rows[c], :] = jnp.broadcast_to(top, (128, HD))

    for part in range(2):
        for e in (1, 3):
            kv_copies[part, e].wait_recv()

    def stripe(ref, k):
        return ref.at[:, pl.ds(pl.multiple_of(k * STRIPE, STRIPE), STRIPE)]

    def piece(p):
        return anc.at[:, pl.ds(pl.multiple_of(colour * STRIPE + p * PIECE, PIECE), PIECE)]

    local_stripe = pltpu.make_async_copy(stripe(kv.at[x], x), stripe(anc, x), loc.at[3])
    far_stripe = rcopy(stripe(kv.at[1], 2), stripe(anc, 2), pass_ss, pass_rs, side(1))

    @pl.when((z == 0) & (x != 2))
    def _():
        local_stripe.start()

    @pl.when(here == NZ)
    def _():
        far_stripe.start()

    lane = lax.broadcasted_iota(jnp.int32, (2, QT, HD), 2)
    n_copies = []
    for pair in ((1, 2), (3, 0)):
        found = {c: (scores(qs[c], kv[1, 0]), scores(qs[c], kv[3, 0])) for c in pair}
        for c in pair:
            old = q_m[rows[c], :][:, :1]
            top = jnp.maximum(jnp.maximum(old, peak_of(found[c][0])), peak_of(found[c][1]))
            n = (
                q_n[rows[c], :] * jnp.exp2((old - top) * SCALE)
                + weigh(found[c][0], top, with_ones(kv[1, 1]))
                + weigh(found[c][1], top, with_ones(kv[3, 1]))
            )
            two = pl.ds(2 * c, 2)
            n_send[two] = (n[:, :HD] / n[:, HD:]).astype(BF16).reshape(2, ROWS, HD)
            lse = (top * SCALE + jnp.log2(n[:, HD:])).reshape(2, GROUP, QT, HD)
            stat = lse[:, 0]
            for g in range(1, GROUP):
                stat = jnp.where(lane == g, lse[:, g], stat)
            st_send[two] = stat
        for d in sorted(2 * c + i for c in pair for i in range(2)):
            if d:
                args = (n_ss.at[0, d], n_rs.at[0, d], zdev(NZ - d))
                n_copies.append(rcopy(st_send.at[d], st_recv.at[d], *args))
                args = (n_ss.at[1, d], n_rs.at[1, d], zdev(NZ - d))
                n_copies.append(rcopy(n_send.at[d], n_recv.at[d], *args))
                n_copies[-2].start()
                n_copies[-1].start()

    scatters = [rcopy(piece(p), piece(p), sc_ss.at[p], sc_rs, zdev(p)) for p in range(1, NZ)]

    @pl.when((z == 0) & (x != 2))
    def _():
        local_stripe.wait()

    @pl.when(here == 2 * NZ)
    def _():
        far_stripe.wait_recv()

    @pl.when(z == 0)
    def _():
        for c in scatters:
            c.start()

    for c in n_copies:
        c.wait_recv()
    st_recv[0] = st_send[0]
    n_recv[0] = n_send[0]
    stats = st_recv[...]
    peak = jnp.max(stats, axis=0)
    share = jnp.exp2(stats - peak[None])
    share = share / jnp.sum(share, axis=0)[None]
    parts = n_recv[...].astype(F32)
    pieces = []
    for g in range(GROUP):
        pieces.append(jnp.sum(parts[:, g * QT : (g + 1) * QT] * share[:, :, g : g + 1], axis=0))
    att[here] = jnp.concatenate(pieces, 0).astype(BF16)

    az = {d: rcopy(att.at[here], att.at[here], az_ss.at[d], az_rs.at[d], zdev(d)) for d in ZS}
    for d in FAR:
        az[d].start()
    @pl.when(z > 0)
    def _():
        rcopy(piece(0), piece(z), sc_ss.at[0], sc_rs, zdev(1)).wait_recv()

    spreads = {d: rcopy(piece(z), piece(z), an_ss.at[d], an_rs.at[d], zdev(d)) for d in ZS}
    for d in FAR:

        @pl.when((z + d) % NZ != 0)
        def _():
            spreads[d].start()

    ax = {}

    def forward(d):
        block = member(NZ - d)
        for e in SIDES:
            dev = side(4) if e == 2 and d % 2 else side(e)
            ax[d, e] = rcopy(att.at[block], att.at[block], ax_ss.at[d, e], ax_rs.at[d, e], dev)
            ax[d, e].start()

    forward(0)

    for d in ZS:
        az[d].wait_recv()
        forward(d)

    @pl.when(z > 0)
    def _():
        for d in ZS:
            spreads[d].wait_recv()

    stripes = []
    for e in (1, 3):
        mine = stripe(anc, colour)
        stripes.append(rcopy(mine, mine, st_ss.at[e], st_rs.at[e], side(e)))
    for e in (2, 4):
        first = colour * STRIPE + (e // 2 - 1) * (STRIPE // 2)
        mine = anc.at[:, pl.ds(pl.multiple_of(first, STRIPE // 2), STRIPE // 2)]
        stripes.append(rcopy(mine, mine, st_ss.at[e], st_rs.at[e], side(e)))
    for c in stripes:
        c.start()

    load_w.wait()
    mine = NCTX * QT // NKV
    po_copies = {}

    def project(first, second):
        blocks = [(x - e + NX) % NX for e in (first, second)]
        lhs = [att[pl.ds(b * NZ, NZ)].astype(F32) for b in blocks]
        acc = jnp.zeros((2 * NZ * QT, no_v.shape[1]), F32)
        for j in range(GROUP // 2):
            pair = [
                jnp.concatenate([a[:, g * QT : (g + 1) * QT].reshape(NZ * QT, HD) for a in lhs], 0)
                for g in (2 * j, 2 * j + 1)
            ]
            acc = acc + jnp.dot(
                jnp.concatenate(pair, 1).astype(BF16),
                w[pl.ds(j * 2 * HD, 2 * HD), :],
                preferred_element_type=F32,
            )
        for i, e in enumerate((first, second)):
            rows = acc[i * NZ * QT : (i + 1) * NZ * QT]
            po[pl.ds(blocks[i] * NC, NC)] = rows.reshape(NC, mine, acc.shape[1]).astype(BF16)
            for c in range(NC):
                dest = blocks[i] * NC + c
                po_copies[e, c] = rcopy(
                    po.at[dest], po_recv.at[head], po_ss.at[e * NC + c], po_rs.at[head], (here, dest)
                )

                @pl.when(dest != head)
                def _():
                    po_copies[e, c].start()

    for d in (0,) + ZS:
        ax[d, 2].wait_recv()
    project(0, 2)
    for d in (0,) + ZS:
        ax[d, 1].wait_recv()
        ax[d, 3].wait_recv()
    project(1, 3)

    for c in stripes:
        c.wait_recv()

    def anchor_head(g, carry):
        cols = pl.ds(pl.multiple_of(g * HD, HD), HD)
        for r in range(4):
            at = pl.ds(r * 128, 128)
            s = scores(cq[at, cols], anc[0])
            top = peak_of(s)
            n = weigh(s, top, with_ones(anc[1]))
            old = own_m[g, at, :]
            peak = jnp.maximum(old, top)
            mine = jnp.where(here > 0, jnp.exp2((old - peak) * SCALE), 1.0)
            theirs = jnp.where(here > 0, jnp.exp2((top - peak) * SCALE), 0.0)
            summed = own_n[g, at, :]
            total = summed[:, HD:] * mine + n[:, HD:] * theirs
            out[at, cols] = ((summed[:, :HD] * mine + n[:, :HD] * theirs) / total).astype(BF16)
        return carry

    half = GROUP * HD // 2
    stores = []

    def anchor_half(i):
        lax.fori_loop(i * GROUP // 2, (i + 1) * GROUP // 2, anchor_head, 0, unroll=4)
        at = pl.ds(i * half, half)
        stores.append(pltpu.make_async_copy(out.at[:, at], co_h.at[0, :, at], loc.at[4 + 3 * i]))
        stores[i].start()

    anchor_half(0)
    anchor_half(1)
    total = po[head].astype(F32)
    for dy, dc in KVS:
        source = (y + dy) % NY * NC + (co + dc) % NC
        rcopy(po.at[0], po_recv.at[source], po_ss.at[0], po_rs.at[source], (here, source)).wait_recv()
        total = total + po_recv[source].astype(F32)
    no_v[...] = total.astype(BF16)

    store_new = pltpu.make_async_copy(no_v, no_h, loc.at[0])
    store_new.start()
    for group in (q_copies, kv_copies, az, ax):
        for c in group.values():
            c.wait_send()
    for c in n_copies:
        c.wait_send()
    for e in range(NX):
        for c in range(NC):

            @pl.when((x - e + NX) % NX * NC + c != head)
            def _():
                po_copies[e, c].wait_send()

    for d in ZS:

        @pl.when((z + d) % NZ != 0)
        def _():
            spreads[d].wait_send()

    for c in stripes:
        c.wait_send()

    @pl.when(here == NZ)
    def _():
        far_stripe.wait_send()

    @pl.when(z == 0)
    def _():
        for c in scatters:
            c.wait_send()

    for c in stores:
        c.wait()
    store_new.wait()


def body(ctx_query, ctx_kv, new_query, new_kv, out_weight):
    any_space = pl.BlockSpec(memory_space=pltpu.HBM)
    cols = out_weight.shape[1]
    mine = NCTX * QT // NKV
    dma = pltpu.SemaphoreType.DMA
    return pl.pallas_call(
        kernel,
        out_shape=(
            jax.ShapeDtypeStruct(ctx_query.shape, BF16),
            jax.ShapeDtypeStruct((mine, cols), BF16),
        ),
        in_specs=[any_space] * 5,
        out_specs=(any_space, any_space),
        scratch_shapes=[
            pltpu.VMEM((BLK, GROUP * HD), BF16),
            pltpu.VMEM((NX, 2, BLK, HD), BF16),
            pltpu.VMEM((GROUP * HD, cols), BF16),
            pltpu.VMEM(new_query.shape, BF16),
            pltpu.VMEM(new_kv.shape, BF16),
            pltpu.VMEM((NX, 2, 16, HD), BF16),
            pltpu.VMEM((NZ, ROWS, HD), BF16),
            pltpu.VMEM((2, BLK, HD), BF16),
            pltpu.VMEM((GROUP, BLK, 2 * HD), F32),
            pltpu.VMEM((GROUP, BLK, HD), F32),
            pltpu.VMEM((BLK, GROUP * HD), BF16),
            pltpu.VMEM((NZ * ROWS, 2 * HD), F32),
            pltpu.VMEM((NZ * ROWS, HD), F32),
            pltpu.VMEM((NZ, ROWS, HD), BF16),
            pltpu.VMEM((NZ, ROWS, HD), BF16),
            pltpu.VMEM((NZ, QT, HD), F32),
            pltpu.VMEM((NZ, QT, HD), F32),
            pltpu.VMEM((NCTX, ROWS, HD), BF16),
            pltpu.VMEM((NKV, mine, cols), BF16),
            pltpu.VMEM((NKV, mine, cols), BF16),
            pltpu.VMEM((mine, cols), BF16),
            dma((8,)),
            dma((NZ,)), dma((NZ,)),
            dma((11,)), dma((11,)),
            dma((2, NZ)), dma((2, NZ)),
            dma((NZ,)), dma((NZ,)),
            dma((NZ,)), dma,
            dma, dma,
            dma((5,)), dma((5,)),
            dma((NZ,)), dma((NZ,)),
            dma((NZ, NX)), dma((NZ, NX)),
            dma((NKV,)), dma((NKV,)),
        ],
        compiler_params=pltpu.CompilerParams(
            collective_id=0, has_side_effects=True, vmem_limit_bytes=60 * 1024 * 1024
        ),
        name="star",
    )(ctx_query, ctx_kv, new_query, new_kv, out_weight)


def solution(mesh):
    return jax.shard_map(
        body,
        mesh=mesh,
        in_specs=(
            P("kv", "ctx", None),
            P(None, "kv", "ctx", None),
            P("kv", "ctx", None),
            P(None, "kv", "ctx", None),
            P("kv", "ctx"),
        ),
        out_specs=(P("kv", "ctx", None), P("kv", "ctx")),
        check_vma=False,
    )
```
